32 devices in a mesh: dp: 8 (over z, x), mp: 4 (over y, core).
Axes of the slice: x: 2, y: 2, z: 4, core: 2. Of those that a mesh axis runs over, the one named last changes fastest.
Arguments:
- frames: bfloat16 [128, 128, 7056], P(('dp', 'mp')), may hold values from -5 to 5
- episode_done: int32 [128, 128], P(('dp', 'mp')), may hold values from 0 to 1, as said below
- target_conv1: bfloat16 [8, 8, 1, 32], replicated, may hold values from -1 to 1
- target_conv2: bfloat16 [4, 4, 32, 64], replicated, may hold values from -0.375 to 0.375
- target_conv3: bfloat16 [3, 3, 64, 64], replicated, may hold values from -0.375 to 0.375
- target_dense: bfloat16 [3136, 512], P('mp'), may hold values from -0.078125 to 0.078125
- predictor_conv1: bfloat16 [8, 8, 1, 32], replicated, may hold values from -1 to 1
- predictor_conv2: bfloat16 [4, 4, 32, 64], replicated, may hold values from -0.375 to 0.375
- predictor_conv3: bfloat16 [3, 3, 64, 64], replicated, may hold values from -0.375 to 0.375
- predictor_dense1: bfloat16 [3136, 512], P('mp', 'dp'), may hold values from -0.15625 to 0.15625
- predictor_dense2: bfloat16 [512, 512], P('dp'), may hold values from -0.375 to 0.375
- predictor_dense3: bfloat16 [512, 512], P('dp'), may hold values from -0.1875 to 0.1875
Outputs:
- embeddings: bfloat16 [128, 128, 512], P(('dp', 'mp'))
- rewards: float32 [128, 128], P(('dp', 'mp'))
- returns: float32 [128, 128], P(('dp', 'mp'))
- grad_conv1: float32 [8, 8, 1, 32], replicated
- grad_conv2: float32 [4, 4, 32, 64], replicated
- grad_conv3: float32 [3, 3, 64, 64], replicated
- grad_dense1: float32 [3136, 512], P('mp', 'dp')
- grad_dense2: float32 [512, 512], P('dp')
- grad_dense3: float32 [512, 512], P('dp')
- frame_grad: bfloat16 [128, 128, 7056], P(('dp', 'mp'))
The draws below stay inside these ranges and needn't reach their ends.
Inputs may be any that keep to these rules, and one draw needn't show every extreme that they name: `episode_done`: 1 marks the last step of an episode; episode lengths differ widely between environments.
All inputs are finite; a program needn't handle non-finite values.
Results may differ from the reference program's by a relative error of at most 0.015.
Values may be sent and summed in bfloat16 or wider, within the bound.
No kernel may reach another device: no remote copies, remote signals or barrier semaphores. Data moves between devices by JAX's collectives and lax.ppermute only.
A program may use at most 320 MiB of HBM per device.

```python
import math
import jax
import jax.numpy as jnp
from jax import lax

PIX = 84
C1 = 32
C2 = 64
C3 = 64
HID = 512
STEPS = 128
ENV_DEV = 4
FEAT = 3136
ENVS = 128
FRAMES = 16384


def draw_episode_done(key, part):
    key = jax.random.fold_in(key, 7)
    key_power, key_ticks = jax.random.split(key)
    power = jax.random.randint(key_power, (ENVS, 1), 2, 10)
    period = jnp.left_shift(jnp.ones_like(power), power)
    ticks = jax.random.randint(key_ticks, (ENVS, STEPS), 0, 1 << 30)
    return (ticks % period == 0).astype(jnp.int32)


def level_of(rng, dims, cuts, low, top_value):
    def one(axis_at, blocks):
        heights = jax.random.uniform(jax.random.fold_in(jax.random.fold_in(rng, 6), axis_at), (blocks,), jnp.float32, low / len(cuts), top_value / len(cuts))
        return jnp.repeat(jnp.exp(heights), dims[axis_at] // blocks).reshape((-1,) + (1,) * (len(dims) - axis_at - 1))

    loudness = one(*cuts[0])
    for cut in cuts[1:]:
        loudness = loudness * one(*cut)
    return loudness


def centred(rng, extent, spread, bound, cuts=(), kind=jnp.bfloat16):
    array = spread * jax.random.normal(rng, extent, jnp.float32)
    if cuts:
        array = array * level_of(rng, extent, cuts, -0.22, 0.18)
    return jnp.clip(array, -bound, bound).astype(kind)


def setup_inputs(seed: int = 0) -> dict:
    keys = jax.random.split(jax.random.key(seed), 13)
    frames = centred(keys[0], (ENVS, STEPS, PIX * PIX), 1.0, 5.0, ((0, 32),))
    episode_done = draw_episode_done(jax.random.fold_in(keys[12], 71), 0)
    target_conv1 = centred(keys[2], (8, 8, 1, C1), 32 ** -0.5, 1.0)
    target_conv2 = centred(keys[3], (4, 4, C1, C2), (8 * C1) ** -0.5, 0.375)
    target_conv3 = centred(keys[4], (3, 3, C2, C3), (9 * C2 // 2) ** -0.5, 0.375)
    target_dense = centred(keys[5], (FEAT, HID), (2 * FEAT) ** -0.5, 0.078125, ((0, 4),))
    predictor_conv1 = centred(keys[6], (8, 8, 1, C1), 32 ** -0.5, 1.0)
    predictor_conv2 = centred(keys[7], (4, 4, C1, C2), (8 * C1) ** -0.5, 0.375)
    predictor_conv3 = centred(keys[8], (3, 3, C2, C3), (9 * C2 // 2) ** -0.5, 0.375)
    predictor_dense1 = centred(keys[9], (FEAT, HID), (FEAT // 2) ** -0.5, 0.15625, ((0, 4), (1, 8)))
    predictor_dense2 = centred(keys[10], (HID, HID), (HID // 2) ** -0.5, 0.375, ((0, 8),))
    predictor_dense3 = centred(keys[11], (HID, HID), (2 * HID) ** -0.5, 0.1875, ((0, 8),))
    return {"frames": frames, "episode_done": episode_done, "target_conv1": target_conv1, "target_conv2": target_conv2, "target_conv3": target_conv3, "target_dense": target_dense, "predictor_conv1": predictor_conv1, "predictor_conv2": predictor_conv2, "predictor_conv3": predictor_conv3, "predictor_dense1": predictor_dense1, "predictor_dense2": predictor_dense2, "predictor_dense3": predictor_dense3}


@jax.custom_vjp
def low(v):
    return lax.optimization_barrier(v.astype(jnp.bfloat16)).astype(jnp.float32)

@jax.custom_vjp
def low_back(v):
    return v

def low_keep(v):
    return (low(v), None)

def low_pass(kept, grad):
    return (grad,)

def back_keep(v):
    return (v, None)

def back_low(kept, grad):
    return (low(grad),)
low.defvjp(low_keep, low_pass)
low_back.defvjp(back_keep, back_low)
GAMMA = 0.99
TRACE = 0.95
HIGH = lax.Precision.HIGHEST

def silu_value(values):
    return values * jax.nn.sigmoid(values)

def conv_forward(pixels, kernel, stride):
    return lax.conv_general_dilated(pixels, kernel, (stride, stride), 'VALID', dimension_numbers=('NHWC', 'HWIO', 'NHWC'), precision=HIGH)

def trunk(pixels, kernels):
    current = pixels
    for kernel, stride in zip(kernels, (4, 2, 1)):
        preact = low_back(conv_forward(current, kernel, stride))
        current = low(silu_value(preact))
    current = low_back(current)
    return current.reshape(current.shape[0], -1)

def head_block(pixels, target_kernels, target_matrix, learner_kernels, dense_one, dense_two, dense_three):
    target_feat = trunk(pixels, target_kernels)
    learner_feat = trunk(pixels, learner_kernels)
    embedding = low_back(jnp.dot(target_feat, target_matrix, precision=HIGH))
    hidden = low_back(jnp.dot(learner_feat, dense_one, precision=HIGH))
    second = low_back(jnp.dot(low(silu_value(hidden)), dense_two, precision=HIGH))
    predicted = low_back(jnp.dot(low(silu_value(second)), dense_three, precision=HIGH))
    differ = predicted - embedding
    return (0.5 * jnp.sum(differ * differ), (embedding, lax.optimization_barrier(jnp.mean(differ * differ, axis=1))))

def discounted(rewards, episode_done):
    keep_going = 1.0 - episode_done.astype(rewards.dtype)

    def step_back(running, inputs):
        reward_now, keep_now = inputs
        running = reward_now + GAMMA * TRACE * keep_now * running
        return (running, running)
    ignored, advantage = lax.scan(step_back, jnp.zeros(rewards.shape[:1], rewards.dtype), (rewards.T, keep_going.T), reverse=True)
    return advantage.T

def reference(frames, episode_done, target_conv1, target_conv2, target_conv3, target_dense, predictor_conv1, predictor_conv2, predictor_conv3, predictor_dense1, predictor_dense2, predictor_dense3):
    target_kernels = tuple((weight.astype(jnp.float32) for weight in (target_conv1, target_conv2, target_conv3)))
    target_matrix = target_dense.astype(jnp.float32)
    pixels = frames.astype(jnp.float32).reshape(ENVS // ENV_DEV, ENV_DEV * STEPS, PIX, PIX, 1)
    learners = tuple((weight.astype(jnp.float32) for weight in (predictor_conv1, predictor_conv2, predictor_conv3, predictor_dense1, predictor_dense2, predictor_dense3)))

    def total_loss(pixel_blocks, kernel_one, kernel_two, kernel_three, dense_one, dense_two, dense_three):

        def one_block(frame_block):
            return head_block(frame_block, target_kernels, target_matrix, (kernel_one, kernel_two, kernel_three), dense_one, dense_two, dense_three)
        losses, extras = lax.map(jax.checkpoint(one_block), pixel_blocks)
        return (jnp.sum(losses), extras)
    total_value, pullback, extras = jax.vjp(total_loss, pixels, *learners, has_aux=True)
    gradients = pullback(jnp.ones((), total_value.dtype))
    grad_scale = 1.0 / math.sqrt(FRAMES)
    embedding, reward_blocks = extras
    rewards = reward_blocks.reshape(ENVS, STEPS)
    returns = discounted(rewards, episode_done)
    frame_grad = gradients[0].reshape(ENVS, STEPS, PIX * PIX).astype(jnp.bfloat16)
    weight_grads = [gradient * grad_scale for gradient in gradients[1:]]
    return (embedding.reshape(ENVS, STEPS, HID).astype(jnp.bfloat16), rewards, returns, weight_grads[0], weight_grads[1], weight_grads[2], weight_grads[3], weight_grads[4], weight_grads[5], frame_grad)
```

```python
import functools
import math

import jax
import jax.numpy as jnp
import numpy as np
from jax import lax
from jax.experimental import pallas as pl
from jax.experimental.pallas import tpu as pltpu
from jax.sharding import PartitionSpec as P

PIX = 84
HID = 512
STEPS = 128
FEAT = 3136
C1 = 32
C2 = 64
C3 = 64
GAMMA = 0.99
TRACE = 0.95

LANES = 256
GROUP = LANES // STEPS
PATCH_ROWS = 336
A1_ROWS = 12800
A1_QROW = 1280
A2_ROWS = 5184
A2P_ROWS = 6400
PAD_ROWS = 7744
BF = jnp.bfloat16
F32 = jnp.float32
VMEM_LIMIT = 60 * 1024 * 1024


def dot_nn(a, b):
    return lax.dot_general(a, b, (((1,), (0,)), ((), ())), preferred_element_type=F32)


def dot_nt(a, b):
    return lax.dot_general(a, b, (((1,), (1,)), ((), ())), preferred_element_type=F32)


def dot_tn(a, b):
    return lax.dot_general(a, b, (((0,), (0,)), ((), ())), preferred_element_type=F32)


def cost(us):
    return pl.CostEstimate(flops=int(us * 1e9), bytes_accessed=int(us * 1e6), transcendentals=0)


def rows(ref, start, size, align=64):
    if not isinstance(start, int):
        start = pl.multiple_of(start, align)
    return ref[pl.ds(start, size), :]


def put(ref, start, size, value, align=64):
    if not isinstance(start, int):
        start = pl.multiple_of(start, align)
    ref[pl.ds(start, size), :] = value


def stack(parts):
    return jnp.concatenate(parts, axis=0)


def silu_pair(z):
    sig = 0.5 * jnp.tanh(0.5 * z) + 0.5
    act = z * sig
    return act, sig + act * (1.0 - sig)


def first_taps():
    out = np.zeros((8, 64, 240), np.float32)
    for q in range(2):
        for dr in range(2):
            for dc in range(2):
                r, c = dr, 2 * q + dc
                for kr in range(8):
                    for kc in range(8):
                        pr, u = divmod(4 * r + kr, 4)
                        pc, v = divmod(4 * c + kc, 4)
                        col = (pr * 5 + pc) * 16 + u * 4 + v
                        out[q * 4 + dr * 2 + dc, kr * 8 + kc, col] = 1.0
    return out


def patch_order():
    out = np.zeros((PATCH_ROWS, PATCH_ROWS), np.float32)
    for pc in range(21):
        for u in range(4):
            for v in range(4):
                out[pc * 16 + u * 4 + v, u * 84 + pc * 4 + v] = 1.0
    return out


def tap_order():
    out = np.zeros((64, 64), np.float32)
    for a in range(2):
        for b in range(2):
            for u in range(4):
                for v in range(4):
                    out[((a * 2 + b) * 4 + u) * 4 + v, (4 * a + u) * 8 + 4 * b + v] = 1.0
    return out


def place(width, block, count):
    out = np.zeros((block, count * width), np.float32)
    for j in range(count):
        for k in range(block):
            out[k, j * width + j * block + k] = 1.0
    return out


def weights_kernel(
    k1t, k2t, k3t, k1p, k2p, k3p, s1, tap, tile, half, quarter, w1, w2, w3a, w3b, v3, v2, v1
):
    for net, (k1, k2, k3) in enumerate(((k1t, k2t, k3t), (k1p, k2p, k3p))):
        one = k1[...]
        for pos in range(8):
            w1[net, pos * 32 : pos * 32 + 32, :] = dot_tn(one, s1[pos]).astype(BF)
        w2[net, :, :] = jnp.zeros((192, 1024), BF)
        for rp in range(2):
            for qq in range(2):
                block = None
                for d in range(4):
                    kr, kc = 2 * rp + d // 2, 2 * qq + d % 2
                    part = dot_tn(
                        k2[(kr * 4 + kc) * 32 : (kr * 4 + kc) * 32 + 32, :],
                        quarter[:, d * 128 : d * 128 + 128],
                    )
                    block = part if block is None else block + part
                for p in range(3):
                    lane = rp * 512 + (p + qq) * 128
                    w2[net, p * 64 : p * 64 + 64, lane : lane + 128] = block.astype(BF)
        turned = [
            [dot_tn(k3[t * 64 : t * 64 + 64, :], half[:, s * 128 : s * 128 + 128]) for s in range(2)]
            for t in range(9)
        ]
        for out, group in ((w3a, 3), (w3b, 2)):
            wide = group + 2
            for p in range(group):
                for j in range((3 * wide + 1) // 2):
                    block = jnp.zeros((64, 128), F32)
                    for s in range(2):
                        k = 2 * j + s
                        r, c = divmod(k, wide)
                        if r < 3 and 0 <= c - p < 3:
                            block = block + turned[r * 3 + c - p][s]
                    lanes = min(128, 3 * wide * 64 - j * 128)
                    out[net, p * 64 : p * 64 + 64, j * 128 : j * 128 + lanes] = block[
                        :, :lanes
                    ].astype(BF)
        spread = dot_nn(k3[...], half[...])
        for p in range(3):
            for j in range(8):
                block = jnp.zeros((64, 128), F32)
                for s in range(2):
                    r, c = divmod(2 * j + s, 5)
                    kr, kc = 2 - r, p + 2 - c
                    if r < 3 and 0 <= kc < 3:
                        t = kr * 3 + kc
                        block = block + spread[t * 64 : t * 64 + 64, s * 128 : s * 128 + 128]
                lanes = min(128, 960 - j * 128)
                v3[net, p * 64 : p * 64 + 64, j * 128 : j * 128 + lanes] = block[:, :lanes].astype(BF)
        spread = dot_nn(k2[...], half[...])
        for d in range(4):
            dr, dc = divmod(d, 2)
            for a in range(2):
                block = jnp.zeros((32, 128), F32)
                for b in range(2):
                    t = (dr + 2 - 2 * a) * 4 + dc + 2 - 2 * b
                    block = block + spread[t * 32 : t * 32 + 32, b * 128 : b * 128 + 128]
                v2[net, d * 32 : d * 32 + 32, a * 128 : a * 128 + 128] = block.astype(BF)
        spread = dot_nn(dot_nn(tap[...], one).astype(BF), tile[...])
        lane = lax.broadcasted_iota(jnp.int32, (16, 128), 1) // 32
        for pr in range(2):
            for pc in range(3):
                for r in range(3):
                    block = jnp.zeros((16, 128), F32)
                    if 0 <= pr + 1 - r < 2:
                        for c in range(4):
                            if 0 <= pc + 1 - c < 2:
                                at = ((pr + 1 - r) * 2 + pc + 1 - c) * 16
                                block = jnp.where(lane == c, spread[at : at + 16, :], block)
                    first = (pr * 3 + pc) * 16
                    at = net * 384 + r * 128
                    v1[first : first + 16, at : at + 128] = block.astype(BF)


def make_weights(target, learner):
    s1 = jnp.asarray(first_taps(), BF)
    tap = jnp.asarray(tap_order(), BF)
    tile = jnp.asarray(np.tile(np.eye(32, dtype=np.float32), (1, 4)), BF)
    half = jnp.asarray(place(128, 64, 2), BF)
    quarter = jnp.asarray(place(128, 32, 4), BF)
    shapes = (
        (2, 256, 240),
        (2, 192, 1024),
        (2, 192, 960),
        (2, 128, 768),
        (2, 192, 960),
        (2, 128, 256),
        (96, 768),
    )
    flat = []
    for k1, k2, k3 in (target, learner):
        flat += [k1.reshape(64, C1), k2.reshape(512, C2), k3.reshape(576, C3)]
    return pl.pallas_call(
        weights_kernel,
        out_shape=[jax.ShapeDtypeStruct(s, BF) for s in shapes],
        compiler_params=pltpu.CompilerParams(vmem_limit_bytes=VMEM_LIMIT),
        name="weights",
    )(*flat, s1, tap, tile, half, quarter)


def forward_kernel(
    x, perm, w1, w2, w3a, w3b, xs, a1, s1, a2, s2, feat, s3, a1_all
):
    net = pl.program_id(0)
    m = pl.program_id(1)

    @pl.when((net == 0) & (m == 0))
    def _():
        for p in range(21):
            part = slice(p * PATCH_ROWS, (p + 1) * PATCH_ROWS)
            block = jnp.concatenate([x[e, part, :] for e in range(GROUP)], axis=1)
            xs[part, :] = dot_nn(perm[...], block).astype(BF)

    for b in range(5):
        window = stack([rows(xs, ((2 * m + r) * 21 + 4 * b) * 16, 80, 16) for r in range(3)])
        act, slope = silu_pair(dot_nn(w1[...], window))
        act = act.astype(BF)
        a1[b * 256 : b * 256 + 256, :] = act
        put(a1_all, m * A1_QROW + b * 256, 256, act, 256)
        s1[b * 256 : b * 256 + 256, :] = slope.astype(BF)

    @pl.when(m >= 1)
    def _():
        i = m - 1
        for g in range(3):
            window = stack([rows(a1_all, ((i + r) * 10 + 3 * g) * 128, 512, 128) for r in range(2)])
            act, slope = silu_pair(dot_nn(w2[...], window))
            put(a2, (i * 10 + 3 * g) * 64, 192, act.astype(BF))
            put(s2, (i * 9 + 3 * g) * 64, 192, slope.astype(BF))
        put(a2, (i * 10 + 9) * 64, 64, jnp.zeros((64, LANES), BF))

    @pl.when(m == 9)
    def _():
        a2[5760:6400, :] = jnp.zeros((640, LANES), BF)

    @pl.when(m >= 3)
    def _():
        i = m - 3
        for c, group in ((0, 3), (3, 2), (5, 2)):
            window = stack(
                [rows(a2, ((i + r) * 10 + c) * 64, (group + 2) * 64) for r in range(3)]
            )
            w = w3a if group == 3 else w3b
            act, slope = silu_pair(dot_nn(w[...], window))
            put(feat, (i * 7 + c) * 64, group * 64, act.astype(BF))
            put(s3, (i * 7 + c) * 64, group * 64, slope.astype(BF))


def forward(chunk, x, perm, w1, w2, w3a, w3b):
    out = lambda *s: jax.ShapeDtypeStruct(s, BF)
    per_net = lambda s: pl.BlockSpec((None, *s), lambda n, m: (n, 0, 0))
    whole = lambda r: pl.BlockSpec((None, r, LANES), lambda n, m: (n, 0, 0))
    return pl.pallas_call(
        forward_kernel,
        grid=(2, 10),
        in_specs=[
            pl.BlockSpec((GROUP, PIX * PIX, STEPS), lambda n, m: (chunk, 0, 0)),
            pl.BlockSpec((PATCH_ROWS, PATCH_ROWS), lambda n, m: (0, 0)),
            per_net(w1.shape[1:]),
            per_net(w2.shape[1:]),
            per_net(w3a.shape[1:]),
            per_net(w3b.shape[1:]),
        ],
        out_specs=[
            pl.BlockSpec((PIX * PIX, LANES), lambda n, m: (0, 0)),
            pl.BlockSpec((A1_QROW, LANES), lambda n, m: (n * m, 0)),
            pl.BlockSpec((None, A1_QROW, LANES), lambda n, m: (n, m, 0)),
            pl.BlockSpec((A2P_ROWS, LANES), lambda n, m: (0, 0)),
            whole(A2_ROWS),
            whole(FEAT),
            whole(FEAT),
        ],
        out_shape=[
            out(PIX * PIX, LANES),
            out(A1_ROWS, LANES),
            out(2, A1_ROWS, LANES),
            out(A2P_ROWS, LANES),
            out(2, A2_ROWS, LANES),
            out(2, FEAT, LANES),
            out(2, FEAT, LANES),
        ],
        scratch_shapes=[pltpu.VMEM((A1_ROWS, LANES), BF)],
        compiler_params=pltpu.CompilerParams(vmem_limit_bytes=VMEM_LIMIT),
        cost_estimate=cost(35),
        name="forward",
    )(x, perm, w1, w2, w3a, w3b)


def embed_kernel(chunks, slabs, ids, *refs):
    feats, dense = refs[:chunks], refs[chunks : chunks + slabs]
    embed, embeddings = refs[chunks + slabs :]
    for c in range(chunks):
        total = None
        for k in range(slabs):
            part = dot_tn(dense[k][...], feats[c][0, ids[k]])
            total = part if total is None else total + part
        embed[c] = total
        embeddings[c * LANES : (c + 1) * LANES, :] = total.astype(BF).T


def embed_call(ids, feats, dense):
    chunks, slabs = len(feats), len(dense)
    full = lambda a: pl.BlockSpec(a.shape, lambda i, s: (0,) * len(a.shape))
    outs = [
        jax.ShapeDtypeStruct((chunks, HID, LANES), F32),
        jax.ShapeDtypeStruct((chunks * LANES, HID), BF),
    ]
    return pl.pallas_call(
        functools.partial(embed_kernel, chunks, slabs),
        grid_spec=pltpu.PrefetchScalarGridSpec(
            num_scalar_prefetch=1,
            grid=(1,),
            in_specs=[
                pl.BlockSpec((1, *f.shape[1:]), lambda i, s: (0, 0, 0, 0)) for f in feats
            ]
            + [full(d) for d in dense],
            out_specs=[full(o) for o in outs],
        ),
        out_shape=outs,
        compiler_params=pltpu.CompilerParams(vmem_limit_bytes=VMEM_LIMIT),
        cost_estimate=cost(5),
        name="embed",
    )(ids, *feats, *dense)


def discounted(rewards, done):
    carry = (GAMMA * TRACE) * (1.0 - done.astype(F32))
    step = lax.broadcasted_iota(jnp.int32, rewards.shape, 1) % STEPS
    carry = jnp.where(step == STEPS - 1, 0.0, carry)
    shift = 1
    while shift < STEPS:
        rewards = rewards + carry * pltpu.roll(rewards, LANES - shift, 1)
        carry = carry * pltpu.roll(carry, LANES - shift, 1)
        shift *= 2
    return rewards


def heads_kernel(chunks, slabs, ids, *refs):
    feats, refs = refs[:chunks], refs[chunks:]
    dense_t, refs = refs[:slabs], refs[slabs:]
    dense1, refs = refs[:slabs], refs[slabs:]
    embed, later, done, refs = refs[0], refs[1], refs[2], refs[3:]
    rewards, returns, refs = refs[0], refs[1], refs[2:]
    gfeats, refs = refs[:chunks], refs[chunks:]
    grads, g_pred, g_second, g_hidden, h1, h2 = refs[:slabs], *refs[slabs:]
    depth = dense1[0].shape[1]
    dense2 = later[:, depth : depth + HID]
    dense3 = later[:, depth + HID : depth + 2 * HID]
    for c in range(chunks):
        lanes = slice(c * LANES, (c + 1) * LANES)
        hidden = None
        for k in range(slabs):
            part = dot_nn(dense1[k][...], feats[c][1, ids[k]])
            hidden = part if hidden is None else hidden + part
        act1, slope1 = silu_pair(hidden)
        act1 = act1.astype(BF)
        second = dot_tn(dense2, act1)
        act2, slope2 = silu_pair(second)
        act2 = act2.astype(BF)
        differ = dot_tn(dense3, act2) - embed[c]
        reward = jnp.sum(differ * differ, axis=0, keepdims=True) * (1.0 / HID)
        rewards[c] = reward
        returns[c] = discounted(reward, done[c])
        pred = differ.astype(BF)
        minus = (-differ).astype(BF)
        deep = (dot_nn(dense3, pred) * slope2).astype(BF)
        low = (dot_nn(dense2, deep) * slope1).astype(BF)
        h1[:, lanes] = act1
        h2[:, lanes] = act2
        g_pred[:, lanes] = pred
        g_second[:, lanes] = deep
        g_hidden[:, lanes] = low
        for k in range(slabs):
            gfeats[c][0, ids[k]] = dot_nn(dense_t[k][...], minus).astype(BF)
            gfeats[c][1, ids[k]] = dot_tn(dense1[k][...], low).astype(BF)
    middle = dot_nt(h1[...], g_second[...]).astype(BF)
    third = dot_nt(h2[...], g_pred[...]).astype(BF)
    share = HID // slabs
    for k in range(slabs):
        both = jnp.concatenate([feats[c][1, ids[k]] for c in range(chunks)], axis=1)
        grads[k][:, :depth] = dot_nt(g_hidden[...], both).astype(BF)
        for q in range(slabs):

            @pl.when(ids[k] == q)
            def _():
                part = slice(q * share, (q + 1) * share)
                grads[k][:, depth : depth + share] = middle[:, part]
                grads[k][:, depth + share : depth + 2 * share] = third[:, part]


def heads(ids, feats, dense_t, dense1, embed, later, done):
    chunks, slabs = len(feats), len(dense1)
    depth = dense1[0].shape[1]
    full = lambda a: pl.BlockSpec(a.shape, lambda i, s: (0,) * len(a.shape))
    line = jax.ShapeDtypeStruct((chunks, 1, LANES), F32)
    grad = jax.ShapeDtypeStruct((HID, depth + 2 * (HID // slabs)), BF)
    outs = [line, line, *[jax.ShapeDtypeStruct(f.shape, BF) for f in feats], *[grad] * slabs]
    ins = [*feats, *dense_t, *dense1, embed, later, done]
    res = pl.pallas_call(
        functools.partial(heads_kernel, chunks, slabs),
        grid_spec=pltpu.PrefetchScalarGridSpec(
            num_scalar_prefetch=1,
            grid=(1,),
            in_specs=[full(a) for a in ins],
            out_specs=[full(o) for o in outs],
            scratch_shapes=[pltpu.VMEM((HID, chunks * LANES), BF)] * 5,
        ),
        out_shape=outs,
        compiler_params=pltpu.CompilerParams(vmem_limit_bytes=VMEM_LIMIT),
        cost_estimate=cost(15),
        name="heads",
    )(ids, *ins)
    return res[0], res[1], res[2 : 2 + chunks], res[2 + chunks :]


def deep_grads(g, s3, s2, v3, d3p, d2p):
    for i in range(7):
        part = slice(i * 448, i * 448 + 448)
        d3p[((i + 2) * 11 + 2) * 64 : ((i + 2) * 11 + 9) * 64, :] = (
            g[part, :].astype(F32) * s3[part, :].astype(F32)
        ).astype(BF)

    @pl.loop(0, 9)
    def _(i):
        for b in range(3):
            window = stack([rows(d3p, ((i + r) * 11 + 3 * b) * 64, 320) for r in range(3)])
            up = dot_nn(v3[...], window)
            slope = rows(s2, (i * 9 + 3 * b) * 64, 192).astype(F32)
            put(d2p, ((i + 1) * 11 + 3 * b + 1) * 64, 192, (up * slope).astype(BF))


def first_grad(m, n, s1, v2, d2p):
    window = stack([rows(d2p, ((m + a) * 11 + n) * 64, 128) for a in range(2)])
    return (dot_nn(v2[...], window) * s1[n * 128 : n * 128 + 128, :].astype(F32)).astype(BF)


def learner_kernel(
    g, s3, s2, s1, a2, a1, xs, v3, v2, s1hot, before, d1, grads, d3p, d2p, sum1, sum2, sum3
):
    m = pl.program_id(0)

    @pl.when(m == 0)
    def _():
        d3p[...] = jnp.zeros_like(d3p)
        d2p[...] = jnp.zeros_like(d2p)
        sum1[...] = jnp.zeros_like(sum1)
        sum2[...] = jnp.zeros_like(sum2)
        sum3[...] = jnp.zeros_like(sum3)
        deep_grads(g, s3, s2, v3, d3p, d2p)

        @pl.loop(0, 4)
        def _(a):
            left = jnp.concatenate(
                [
                    stack([rows(d3p, ((2 * a + 2 + r) * 11 + 2 * b + 2) * 64, 128) for r in range(2)])
                    for b in range(4)
                ],
                axis=1,
            )
            right = jnp.concatenate(
                [
                    stack([rows(a2, ((2 * a + r) * 10 + 2 * b) * 64, 256) for r in range(4)])
                    for b in range(4)
                ],
                axis=1,
            )
            sum3[...] += dot_nt(left, right)

    for n in range(10):
        d1[n * 128 : n * 128 + 128, :] = first_grad(m, n, s1, v2, d2p)

    left = jnp.concatenate(
        [
            stack([rows(d2p, ((m + r) * 11 + 2 * b) * 64, 192) for r in range(2)])
            for b in range(5)
        ],
        axis=1,
    )
    right = jnp.concatenate([a1[b * 256 : b * 256 + 256, :] for b in range(5)], axis=1)
    sum2[...] += dot_nt(left, right)
    left = jnp.concatenate([d1[b * 256 : b * 256 + 256, :] for b in range(5)], axis=1)
    right = jnp.concatenate(
        [
            stack([rows(xs, ((2 * m + r) * 21 + 4 * b) * 16, 80, 16) for r in range(3)])
            for b in range(5)
        ],
        axis=1,
    )
    sum1[...] += dot_nt(left, right)

    @pl.when(m == 9)
    def _():
        grads[...] = before[...]
        total = jnp.zeros((64, 32), F32)
        for pos in range(8):
            block = sum1[pos * 32 : pos * 32 + 32, :]
            high = block.astype(BF)
            rest = block - high.astype(F32)
            mid = rest.astype(BF)
            low = (rest - mid.astype(F32)).astype(BF)
            hot = s1hot[pos]
            total = total + (dot_nt(hot, high) + (dot_nt(hot, mid) + dot_nt(hot, low)))
        grads[640:704, 0:32] += total
        for rp in range(2):
            for qq in range(2):
                block = None
                for q in range(2):
                    dj = q + 1 - qq
                    at = ((1 - rp) * 3 + dj) * 64
                    part = sum2[at : at + 64, q * 128 : q * 128 + 128]
                    block = part if block is None else block + part
                grads[(rp * 2 + qq) * 64 : (rp * 2 + qq) * 64 + 64, :] += block
        for kr in range(3):
            block = None
            for pr in range(2):
                for pc in range(2):
                    at = (pr * 2 + pc) * 64
                    lane = (pr + kr) * 256 + pc * 64
                    part = sum3[at : at + 64, lane : lane + 192]
                    block = part if block is None else block + part
            grads[256 + kr * 64 : 320 + kr * 64, :] += block[:, :128]
            grads[448 + kr * 64 : 512 + kr * 64, 0:64] += block[:, 128:]


PACKED = 768


def learner_backward(gfeat, s3, s2, s1, a2, a1, xs, v3, v2, before):
    mine = lambda r: pl.BlockSpec((None, r, LANES), lambda m: (1, 0, 0))
    fixed = lambda s: pl.BlockSpec(s, lambda m: (0,) * len(s))
    qrow = pl.BlockSpec((A1_QROW, LANES), lambda m: (m, 0))
    s1hot = jnp.asarray(first_taps(), BF)
    return pl.pallas_call(
        learner_kernel,
        grid=(10,),
        in_specs=[
            mine(FEAT),
            mine(FEAT),
            mine(A2_ROWS),
            pl.BlockSpec((None, A1_QROW, LANES), lambda m: (1, m, 0)),
            fixed((A2P_ROWS, LANES)),
            qrow,
            fixed((PIX * PIX, LANES)),
            pl.BlockSpec((None, *v3.shape[1:]), lambda m: (1, 0, 0)),
            pl.BlockSpec((None, *v2.shape[1:]), lambda m: (1, 0, 0)),
            fixed(s1hot.shape),
            fixed((PACKED, 128)),
        ],
        out_specs=[qrow, fixed((PACKED, 128))],
        out_shape=[
            jax.ShapeDtypeStruct((A1_ROWS, LANES), BF),
            jax.ShapeDtypeStruct((PACKED, 128), F32),
        ],
        scratch_shapes=[
            pltpu.VMEM((PAD_ROWS, LANES), BF),
            pltpu.VMEM((PAD_ROWS, LANES), BF),
            pltpu.VMEM((256, 240), F32),
            pltpu.VMEM((384, 256), F32),
            pltpu.VMEM((256, 1024), F32),
        ],
        compiler_params=pltpu.CompilerParams(vmem_limit_bytes=VMEM_LIMIT),
        cost_estimate=cost(25),
        name="learner_backward",
    )(gfeat, s3, s2, s1, a2, a1, xs, v3, v2, s1hot, before)


def pixel_kernel(g, s3, s2, s1, d1p, v3, v2, v1, perm, *refs):
    out, d3p, d2p, band, dxs = refs[-5:]
    m = pl.program_id(0)

    @pl.when(m == 0)
    def _():
        d3p[...] = jnp.zeros_like(d3p)
        d2p[...] = jnp.zeros_like(d2p)
        band[...] = jnp.zeros_like(band)
        deep_grads(g, s3, s2, v3, d3p, d2p)

    @pl.when(m > 0)
    def _():
        band[0, 0] = band[2, 0]
        band[0, 1] = band[2, 1]

    for n in range(10):
        mine = first_grad(m, n, s1, v2, d2p)
        theirs = d1p[n * 128 : n * 128 + 128, :]
        for dr in range(2):
            at = slice((2 * n + 1) * 32, (2 * n + 3) * 32)
            band[1 + dr, 0, at, :] = mine[dr * 64 : dr * 64 + 64, :]
            band[1 + dr, 1, at, :] = theirs[dr * 64 : dr * 64 + 64, :]

    for b in range(7):
        at = slice(3 * b * 32, 3 * b * 32 + 128)
        window = stack([band[r, net, at, :] for net in range(2) for r in range(3)])
        dx = dot_nn(v1[...], window).astype(BF)
        put(dxs, (2 * m * 21 + 3 * b) * 16, 48, dx[:48], 16)
        put(dxs, ((2 * m + 1) * 21 + 3 * b) * 16, 48, dx[48:], 16)

    @pl.when(m == 9)
    def _():
        w = jnp.concatenate([v1[:48, 0:128], v1[:48, 384:512]], axis=1)
        for b in range(7):
            at = slice(3 * b * 32, 3 * b * 32 + 128)
            window = stack([band[2, net, at, :] for net in range(2)])
            put(dxs, (20 * 21 + 3 * b) * 16, 48, dot_nn(w, window).astype(BF), 16)
        for p in range(21):
            part = slice(p * PATCH_ROWS, (p + 1) * PATCH_ROWS)
            block = dot_tn(perm[...], dxs[part, :]).astype(BF)
            for e in range(GROUP):
                out[e, part, :] = block[:, e * STEPS : (e + 1) * STEPS]


def pixel_backward(chunk, envs, gfeat, s3, s2, s1, d1p, v3, v2, v1, perm, before):
    mine = lambda r: pl.BlockSpec((None, r, LANES), lambda m: (0, 0, 0))
    fixed = lambda s: pl.BlockSpec(s, lambda m: (0,) * len(s))
    ins = [gfeat, s3, s2, s1, d1p, v3, v2, v1, perm]
    specs = [
        mine(FEAT),
        mine(FEAT),
        mine(A2_ROWS),
        pl.BlockSpec((None, A1_QROW, LANES), lambda m: (0, m, 0)),
        pl.BlockSpec((A1_QROW, LANES), lambda m: (m, 0)),
        pl.BlockSpec((None, *v3.shape[1:]), lambda m: (0, 0, 0)),
        pl.BlockSpec((None, *v2.shape[1:]), lambda m: (0, 0, 0)),
        fixed(v1.shape),
        fixed(perm.shape),
    ]
    aliases = {}
    if before is not None:
        aliases = {len(ins): 0}
        ins.append(before)
        specs.append(pl.BlockSpec(memory_space=pl.ANY))
    return pl.pallas_call(
        pixel_kernel,
        grid=(10,),
        in_specs=specs,
        out_specs=pl.BlockSpec((GROUP, PIX * PIX, STEPS), lambda m: (chunk, 0, 0)),
        out_shape=jax.ShapeDtypeStruct((envs, PIX * PIX, STEPS), BF),
        scratch_shapes=[
            pltpu.VMEM((PAD_ROWS, LANES), BF),
            pltpu.VMEM((PAD_ROWS, LANES), BF),
            pltpu.VMEM((3, 2, 22 * 32, LANES), BF),
            pltpu.VMEM((PIX * PIX, LANES), BF),
        ],
        input_output_aliases=aliases,
        compiler_params=pltpu.CompilerParams(vmem_limit_bytes=VMEM_LIMIT),
        cost_estimate=cost(20),
        name="pixel_backward",
    )(*ins)


def shards(
    frames,
    episode_done,
    target_conv1,
    target_conv2,
    target_conv3,
    target_dense,
    predictor_conv1,
    predictor_conv2,
    predictor_conv3,
    predictor_dense1,
    predictor_dense2,
    predictor_dense3,
):
    everyone = ("dp", "mp")
    dp, mp = lax.axis_size("dp"), lax.axis_size("mp")
    envs_here = frames.shape[0]
    count = envs_here * STEPS
    chunks = count // LANES
    grad_scale = 1.0 / math.sqrt(count * dp * mp)
    cores = 2 if mp % 2 == 0 else 1
    chips = mp // cores
    depth = target_dense.shape[0]

    def from_chip(value, j):
        pairs = [(i, ((i // cores + j) % chips) * cores + i % cores) for i in range(mp)]
        return lax.ppermute(value, "mp", pairs)

    def other_core(value):
        return lax.ppermute(value, "mp", [(i, i ^ 1) for i in range(mp)])

    here = lax.axis_index("mp")
    chip, core = here // cores, here % cores
    ids = jnp.stack(
        [
            ((chip + chips - j) % chips) * cores + (core + k) % cores
            for k in range(cores)
            for j in range(chips)
        ]
    ).astype(jnp.int32)

    x = frames.swapaxes(1, 2)
    perm = jnp.asarray(patch_order(), BF)
    packed = jnp.concatenate([predictor_dense1.T, predictor_dense2, predictor_dense3], axis=1)
    later = lax.all_gather(packed, "dp", axis=0, tiled=True)
    dense_t = [target_dense] + [from_chip(target_dense, j) for j in range(1, chips)]
    w1, w2, w3a, w3b, v3, v2, v1 = make_weights(
        (target_conv1, target_conv2, target_conv3),
        (predictor_conv1, predictor_conv2, predictor_conv3),
    )
    saved = [forward(0, x, perm, w1, w2, w3a, w3b)]
    tie = lax.optimization_barrier((x, later, tuple(dense_t), saved[0][0]))
    x, later, dense_t = tie[0], tie[1], list(tie[2])
    saved[0] = (tie[3], *saved[0][1:])
    if cores == 2:
        dense_t += [other_core(d) for d in dense_t]
    mine = later[:, :depth]
    dense1 = [mine] + [from_chip(mine, j) for j in range(1, chips)]
    for c in range(1, chunks):
        saved.append(forward(c, x, perm, w1, w2, w3a, w3b))
    if cores == 2:
        tie = lax.optimization_barrier((tuple(dense1), tuple(dense_t), saved[-1][5]))
        dense1, dense_t = list(tie[0]), list(tie[1])
        saved[-1] = (*saved[-1][:5], tie[2], saved[-1][6])
        dense1 += [other_core(d) for d in dense1]
    feats = [sv[5].reshape(2, mp, depth, LANES) for sv in saved]
    embed, embeddings = embed_call(ids, feats, dense_t)
    rewards, returns, gfeats, grads = heads(
        ids, feats, dense_t, dense1, embed, later, episode_done.reshape(chunks, 1, LANES)
    )
    gfeats = [g.reshape(2, FEAT, LANES) for g in gfeats]

    kept, sent = grads[:chips], grads[chips:]
    got = [other_core(g) for g in sent]
    first = []
    small = jnp.zeros((PACKED, 128), F32)
    for c in range(chunks):
        xs, a1, s1, a2, s2, feat, s3 = saved[c]
        grad1, small = learner_backward(gfeats[c], s3, s2, s1, a2, a1, xs, v3, v2, small)
        first.append(grad1)
        if c == 0:
            if sent:
                kept = [(a.astype(F32) + b.astype(F32)).astype(BF) for a, b in zip(kept, got)]
            tie = lax.optimization_barrier((tuple(kept), small))
            kept, small = list(tie[0]), tie[1]
            got = [from_chip(kept[j], chips - j) for j in range(1, chips)]
    total = kept[0].astype(F32)
    for g in got:
        total = total + g.astype(F32)
    total = total.astype(BF).reshape(dp, HID // dp, -1)
    total, small, gfeats[0] = lax.optimization_barrier((total, small, gfeats[0]))
    total = lax.all_to_all(total, "dp", split_axis=0, concat_axis=0, tiled=True)
    small = small.reshape(dp * mp, PACKED // (dp * mp), 128)
    small = lax.all_to_all(small, everyone, split_axis=0, concat_axis=0, tiled=True)
    frame_grad = None
    for c in range(chunks):
        xs, a1, s1, a2, s2, feat, s3 = saved[c]
        frame_grad = pixel_backward(
            c, envs_here, gfeats[c], s3, s2, s1, first[c], v3, v2, v1, perm, frame_grad
        )
        if c == 0:
            share = jnp.sum(small, axis=0)
            share, frame_grad = lax.optimization_barrier((share, frame_grad))
            share = jnp.broadcast_to(share[None], (dp * mp, *share.shape))
            small = lax.all_to_all(share, everyone, split_axis=0, concat_axis=0, tiled=True)
    total = jnp.sum(total.astype(F32), axis=0)
    d1 = total[:, :depth] * grad_scale
    tail = total[:, depth:].astype(BF)
    tail = lax.all_to_all(
        jnp.broadcast_to(tail[None], (mp, *tail.shape)), "mp", split_axis=0, concat_axis=0, tiled=True
    )
    tail = tail.astype(F32) * grad_scale
    width = HID // mp
    d2 = jnp.concatenate([tail[k, :, :width] for k in range(mp)], axis=1)
    d3 = jnp.concatenate([tail[k, :, width:] for k in range(mp)], axis=1)

    small = small.reshape(PACKED, 128) * grad_scale
    e1 = small[640:704, :C1].reshape(8, 8, 1, C1)
    e2 = small[:256].reshape(2, 2, C2, 2, 2, C1).transpose(0, 3, 1, 4, 5, 2)
    e3 = jnp.concatenate([small[256:448], small[448:640, :64]], axis=1)
    e3 = e3.reshape(3, C3, 3, C2).transpose(0, 2, 3, 1)
    return (
        embeddings.reshape(envs_here, STEPS, HID),
        rewards.reshape(envs_here, STEPS),
        returns.reshape(envs_here, STEPS),
        e1,
        e2.reshape(4, 4, C1, C2),
        e3,
        d1.T,
        d2,
        d3,
        frame_grad.swapaxes(1, 2),
    )


def solution(mesh):
    placed = (
        P(("dp", "mp"), None, None),
        P(("dp", "mp"), None),
        P(),
        P(),
        P(),
        P("mp", None),
        P(),
        P(),
        P(),
        P("mp", "dp"),
        P("dp", None),
        P("dp", None),
    )
    return jax.shard_map(
        shards,
        mesh=mesh,
        in_specs=placed,
        out_specs=(
            P(("dp", "mp"), None, None),
            P(("dp", "mp"), None),
            P(("dp", "mp"), None),
            P(),
            P(),
            P(),
            P("mp", "dp"),
            P("dp", None),
            P("dp", None),
            P(("dp", "mp"), None, None),
        ),
        check_vma=False,
    )
```

```python
import functools
import math

import jax
import jax.numpy as jnp
import numpy as np
from jax import lax
from jax.experimental import pallas as pl
from jax.experimental.pallas import tpu as pltpu
from jax.sharding import PartitionSpec as P

PIX = 84
HID = 512
STEPS = 128
FEAT = 3136
C1 = 32
C2 = 64
C3 = 64
GAMMA = 0.99
TRACE = 0.95

LANES = 256
GROUP = LANES // STEPS
PATCH_ROWS = 336
A1_ROWS = 12800
A1_QROW = 1280
A2_ROWS = 5184
A2P_ROWS = 6400
PAD_ROWS = 7744
BF = jnp.bfloat16
F32 = jnp.float32
VMEM_LIMIT = 60 * 1024 * 1024


def dot_nn(a, b):
    return lax.dot_general(a, b, (((1,), (0,)), ((), ())), preferred_element_type=F32)


def dot_nt(a, b):
    return lax.dot_general(a, b, (((1,), (1,)), ((), ())), preferred_element_type=F32)


def dot_tn(a, b):
    return lax.dot_general(a, b, (((0,), (0,)), ((), ())), preferred_element_type=F32)


def cost(us):
    return pl.CostEstimate(flops=int(us * 1e9), bytes_accessed=int(us * 1e6), transcendentals=0)


def waits(others):
    return [pl.BlockSpec(memory_space=pl.ANY)] * len(others)


def after(value, *others):
    def kernel(*refs):
        del refs

    return pl.pallas_call(
        kernel,
        in_specs=waits((value, *others)),
        out_specs=pl.BlockSpec(memory_space=pl.ANY),
        out_shape=jax.ShapeDtypeStruct(value.shape, value.dtype),
        input_output_aliases={0: 0},
        cost_estimate=cost(0),
        name="after",
    )(value, *others)


def rows(ref, start, size, align=64):
    if not isinstance(start, int):
        start = pl.multiple_of(start, align)
    return ref[pl.ds(start, size), :]


def put(ref, start, size, value, align=64):
    if not isinstance(start, int):
        start = pl.multiple_of(start, align)
    ref[pl.ds(start, size), :] = value


def stack(parts):
    return jnp.concatenate(parts, axis=0)


def silu_pair(z):
    sig = 0.5 * jnp.tanh(0.5 * z) + 0.5
    act = z * sig
    return act, sig + act * (1.0 - sig)


def first_taps():
    out = np.zeros((8, 64, 240), np.float32)
    for q in range(2):
        for dr in range(2):
            for dc in range(2):
                r, c = dr, 2 * q + dc
                for kr in range(8):
                    for kc in range(8):
                        pr, u = divmod(4 * r + kr, 4)
                        pc, v = divmod(4 * c + kc, 4)
                        col = (pr * 5 + pc) * 16 + u * 4 + v
                        out[q * 4 + dr * 2 + dc, kr * 8 + kc, col] = 1.0
    return out


def patch_order():
    out = np.zeros((PATCH_ROWS, PATCH_ROWS), np.float32)
    for pc in range(21):
        for u in range(4):
            for v in range(4):
                out[pc * 16 + u * 4 + v, u * 84 + pc * 4 + v] = 1.0
    return out


def tap_order():
    out = np.zeros((64, 64), np.float32)
    for a in range(2):
        for b in range(2):
            for u in range(4):
                for v in range(4):
                    out[((a * 2 + b) * 4 + u) * 4 + v, (4 * a + u) * 8 + 4 * b + v] = 1.0
    return out


def place(width, block, count):
    out = np.zeros((block, count * width), np.float32)
    for j in range(count):
        for k in range(block):
            out[k, j * width + j * block + k] = 1.0
    return out


def weights_kernel(
    k1t, k2t, k3t, k1p, k2p, k3p, s1, tap, tile, half, quarter, w1, w2, w3a, w3b, v3, v2, v1
):
    for net, (k1, k2, k3) in enumerate(((k1t, k2t, k3t), (k1p, k2p, k3p))):
        one = k1[...]
        for pos in range(8):
            w1[net, pos * 32 : pos * 32 + 32, :] = dot_tn(one, s1[pos]).astype(BF)
        w2[net, :, :] = jnp.zeros((192, 1024), BF)
        for rp in range(2):
            for qq in range(2):
                block = None
                for d in range(4):
                    kr, kc = 2 * rp + d // 2, 2 * qq + d % 2
                    part = dot_tn(
                        k2[(kr * 4 + kc) * 32 : (kr * 4 + kc) * 32 + 32, :],
                        quarter[:, d * 128 : d * 128 + 128],
                    )
                    block = part if block is None else block + part
                for p in range(3):
                    lane = rp * 512 + (p + qq) * 128
                    w2[net, p * 64 : p * 64 + 64, lane : lane + 128] = block.astype(BF)
        turned = [
            [dot_tn(k3[t * 64 : t * 64 + 64, :], half[:, s * 128 : s * 128 + 128]) for s in range(2)]
            for t in range(9)
        ]
        for out, group in ((w3a, 3), (w3b, 2)):
            wide = group + 2
            for p in range(group):
                for j in range((3 * wide + 1) // 2):
                    block = jnp.zeros((64, 128), F32)
                    for s in range(2):
                        k = 2 * j + s
                        r, c = divmod(k, wide)
                        if r < 3 and 0 <= c - p < 3:
                            block = block + turned[r * 3 + c - p][s]
                    lanes = min(128, 3 * wide * 64 - j * 128)
                    out[net, p * 64 : p * 64 + 64, j * 128 : j * 128 + lanes] = block[
                        :, :lanes
                    ].astype(BF)
        spread = dot_nn(k3[...], half[...])
        for p in range(3):
            for j in range(8):
                block = jnp.zeros((64, 128), F32)
                for s in range(2):
                    r, c = divmod(2 * j + s, 5)
                    kr, kc = 2 - r, p + 2 - c
                    if r < 3 and 0 <= kc < 3:
                        t = kr * 3 + kc
                        block = block + spread[t * 64 : t * 64 + 64, s * 128 : s * 128 + 128]
                lanes = min(128, 960 - j * 128)
                v3[net, p * 64 : p * 64 + 64, j * 128 : j * 128 + lanes] = block[:, :lanes].astype(BF)
        spread = dot_nn(k2[...], half[...])
        for d in range(4):
            dr, dc = divmod(d, 2)
            for a in range(2):
                block = jnp.zeros((32, 128), F32)
                for b in range(2):
                    t = (dr + 2 - 2 * a) * 4 + dc + 2 - 2 * b
                    block = block + spread[t * 32 : t * 32 + 32, b * 128 : b * 128 + 128]
                v2[net, d * 32 : d * 32 + 32, a * 128 : a * 128 + 128] = block.astype(BF)
        spread = dot_nn(dot_nn(tap[...], one).astype(BF), tile[...])
        lane = lax.broadcasted_iota(jnp.int32, (16, 128), 1) // 32
        for pr in range(4):
            for pc in range(3):
                for r in range(5):
                    block = jnp.zeros((16, 128), F32)
                    if 0 <= pr + 1 - r < 2:
                        for c in range(4):
                            if 0 <= pc + 1 - c < 2:
                                at = ((pr + 1 - r) * 2 + pc + 1 - c) * 16
                                block = jnp.where(lane == c, spread[at : at + 16, :], block)
                    first = (pr * 3 + pc) * 16
                    at = net * 640 + r * 128
                    v1[first : first + 16, at : at + 128] = block.astype(BF)


def make_weights(target, learner):
    s1 = jnp.asarray(first_taps(), BF)
    tap = jnp.asarray(tap_order(), BF)
    tile = jnp.asarray(np.tile(np.eye(32, dtype=np.float32), (1, 4)), BF)
    half = jnp.asarray(place(128, 64, 2), BF)
    quarter = jnp.asarray(place(128, 32, 4), BF)
    shapes = (
        (2, 256, 240),
        (2, 192, 1024),
        (2, 192, 960),
        (2, 128, 768),
        (2, 192, 960),
        (2, 128, 256),
        (192, 1280),
    )
    flat = []
    for k1, k2, k3 in (target, learner):
        flat += [k1.reshape(64, C1), k2.reshape(512, C2), k3.reshape(576, C3)]
    return pl.pallas_call(
        weights_kernel,
        out_shape=[jax.ShapeDtypeStruct(s, BF) for s in shapes],
        compiler_params=pltpu.CompilerParams(vmem_limit_bytes=VMEM_LIMIT),
        name="weights",
    )(*flat, s1, tap, tile, half, quarter)


def forward_kernel(x, perm, w1, w2, w3a, w3b, *refs):
    xs_out, a1_out, s1_out, a2_out, s2_out, feat_out, s3_out = refs[-15:-8]
    xs, a1, s1, a2, s2, feat, s3, sems = refs[-8:]

    def keep(buffer, out, index):
        return pltpu.make_async_copy(buffer, out, sems.at[index])

    def both(net, index, *pairs):
        for k, (buffer, out) in enumerate(pairs):
            keep(buffer.at[net], out.at[net], index + k).start()

    @pl.loop(0, 7)
    def _(p):
        for k in range(3):
            part = pl.ds(pl.multiple_of((3 * p + k) * PATCH_ROWS, 16), PATCH_ROWS)
            block = jnp.concatenate([x[e, part, :] for e in range(GROUP)], axis=1)
            xs[part, :] = dot_nn(perm[...], block).astype(BF)

    keep(xs, xs_out, 0).start()
    for i in range(9):
        a2[(i * 10 + 9) * 64 : (i * 10 + 10) * 64, :] = jnp.zeros((64, LANES), BF)
    a2[5760:6400, :] = jnp.zeros((640, LANES), BF)

    def first(t):
        net, v = t // 5, t % 5
        for q in range(2):
            m = 2 * v + q
            for b in range(5):
                window = stack([rows(xs, ((2 * m + r) * 21 + 4 * b) * 16, 80, 16) for r in range(3)])
                act, slope = silu_pair(dot_nn(w1[net], window))
                put(a1, m * A1_QROW + b * 256, 256, act.astype(BF), 256)
                put(s1.at[net], m * A1_QROW + b * 256, 256, slope.astype(BF), 256)

    def second(t):
        net, v = (t - 1) // 5, (t - 1) % 5
        for q in range(2):
            i = jnp.maximum(2 * v - 1 + q, 0)
            for g in range(3):
                window = stack([rows(a1, ((i + r) * 10 + 3 * g) * 128, 512, 128) for r in range(2)])
                act, slope = silu_pair(dot_nn(w2[net], window))
                put(a2, (i * 10 + 3 * g) * 64, 192, act.astype(BF))
                put(s2.at[net], (i * 9 + 3 * g) * 64, 192, slope.astype(BF))

    def third(t):
        net, v = (t - 3) // 5, (t - 3) % 5
        for q in range(2):
            i = jnp.maximum(2 * v - 1 + q, 0)
            for c, group in ((0, 3), (3, 2), (5, 2)):
                window = stack(
                    [rows(a2, ((i + r) * 10 + c) * 64, (group + 2) * 64) for r in range(3)]
                )
                w = w3a if group == 3 else w3b
                act, slope = silu_pair(dot_nn(w[net], window))
                put(feat.at[net], (i * 7 + c) * 64, group * 64, act.astype(BF))
                put(s3.at[net], (i * 7 + c) * 64, group * 64, slope.astype(BF))

    early_a2, late_a2 = pl.ds(0, 7 * 640), pl.ds(7 * 640, 3 * 640)
    early_s2, late_s2 = pl.ds(0, 7 * 576), pl.ds(7 * 576, 2 * 576)
    early, late = pl.ds(0, 5 * 448), pl.ds(5 * 448, 2 * 448)

    @pl.loop(0, 12)
    def _(t):
        @pl.when(t == 0)
        def _():
            first(t)

        @pl.when((t == 1) | (t == 2) | (t == 7))
        def _():
            second(t)
            first(t)

        @pl.when(((t >= 3) & (t <= 6)) | (t == 8) | (t == 9))
        def _():
            third(t)
            second(t)
            first(t)

        @pl.when(t == 10)
        def _():
            keep(a2.at[early_a2], a2_out.at[early_a2], 6).start()
            keep(s2.at[1, early_s2], s2_out.at[1, early_s2], 3).start()
            third(t)
            second(t)

        @pl.when(t == 11)
        def _():
            keep(a2.at[late_a2], a2_out.at[late_a2], 6).start()
            keep(s2.at[1, late_s2], s2_out.at[1, late_s2], 3).start()
            keep(feat.at[1, early], feat_out.at[1, early], 4).start()
            keep(s3.at[1, early], s3_out.at[1, early], 5).start()
            third(t)

        @pl.when(t == 7)
        def _():
            both(0, 3, (s2, s2_out), (feat, feat_out), (s3, s3_out))

        @pl.when(t < 10)
        def _():
            part = pl.ds(pl.multiple_of((t % 5) * 2 * A1_QROW, 256), 2 * A1_QROW)
            keep(s1.at[t // 5, part], s1_out.at[t // 5, part], 2).start()

        @pl.when((t >= 5) & (t < 10))
        def _():
            part = pl.ds(pl.multiple_of((t % 5) * 2 * A1_QROW, 256), 2 * A1_QROW)
            keep(a1.at[part], a1_out.at[part], 1).start()

    keep(feat.at[1, late], feat_out.at[1, late], 4).start()
    keep(s3.at[1, late], s3_out.at[1, late], 5).start()
    for k, (buffer, out) in enumerate(
        (
            (xs, xs_out), (a1, a1_out), (s1, s1_out), (s2, s2_out), (feat, feat_out), (s3, s3_out),
            (a2, a2_out),
        )
    ):
        keep(buffer, out, k).wait()


def forward(chunk, x, perm, w1, w2, w3a, w3b, deps=()):
    shapes = (
        (PIX * PIX, LANES),
        (A1_ROWS, LANES),
        (2, A1_ROWS, LANES),
        (A2P_ROWS, LANES),
        (2, A2_ROWS, LANES),
        (2, FEAT, LANES),
        (2, FEAT, LANES),
    )
    fixed = lambda a: pl.BlockSpec(a.shape, lambda i: (0,) * len(a.shape))
    return pl.pallas_call(
        forward_kernel,
        grid=(1,),
        in_specs=[pl.BlockSpec((GROUP, PIX * PIX, STEPS), lambda i: (chunk, 0, 0))]
        + [fixed(a) for a in (perm, w1, w2, w3a, w3b)]
        + waits(deps),
        out_specs=[pl.BlockSpec(memory_space=pl.ANY)] * len(shapes),
        out_shape=[jax.ShapeDtypeStruct(s, BF) for s in shapes],
        scratch_shapes=[pltpu.VMEM(s, BF) for s in shapes] + [pltpu.SemaphoreType.DMA((7,))],
        compiler_params=pltpu.CompilerParams(vmem_limit_bytes=VMEM_LIMIT),
        cost_estimate=cost(25),
        name="forward",
    )(x, perm, w1, w2, w3a, w3b, *deps)


def embed_kernel(chunks, slabs, ids, *refs):
    feats, dense = refs[:chunks], refs[chunks : chunks + slabs]
    embed, embeddings = refs[-2:]
    for c in range(chunks):
        total = None
        for k in range(slabs):
            part = dot_tn(dense[k][...], feats[c][0, ids[k]])
            total = part if total is None else total + part
        embed[c] = total
        embeddings[c * LANES : (c + 1) * LANES, :] = total.astype(BF).T


def embed_call(ids, feats, dense, deps=()):
    chunks, slabs = len(feats), len(dense)
    full = lambda a: pl.BlockSpec(a.shape, lambda i, s: (0,) * len(a.shape))
    outs = [
        jax.ShapeDtypeStruct((chunks, HID, LANES), F32),
        jax.ShapeDtypeStruct((chunks * LANES, HID), BF),
    ]
    return pl.pallas_call(
        functools.partial(embed_kernel, chunks, slabs),
        grid_spec=pltpu.PrefetchScalarGridSpec(
            num_scalar_prefetch=1,
            grid=(1,),
            in_specs=[
                pl.BlockSpec((1, *f.shape[1:]), lambda i, s: (0, 0, 0, 0)) for f in feats
            ]
            + [full(d) for d in dense]
            + waits(deps),
            out_specs=[full(o) for o in outs],
        ),
        out_shape=outs,
        compiler_params=pltpu.CompilerParams(vmem_limit_bytes=VMEM_LIMIT),
        cost_estimate=cost(5),
        name="embed",
    )(ids, *feats, *dense, *deps)


def discounted(rewards, done):
    carry = (GAMMA * TRACE) * (1.0 - done.astype(F32))
    step = lax.broadcasted_iota(jnp.int32, rewards.shape, 1) % STEPS
    carry = jnp.where(step == STEPS - 1, 0.0, carry)
    shift = 1
    while shift < STEPS:
        rewards = rewards + carry * pltpu.roll(rewards, LANES - shift, 1)
        carry = carry * pltpu.roll(carry, LANES - shift, 1)
        shift *= 2
    return rewards


def heads_kernel(chunks, slabs, depth, ids, *refs):
    feats, refs = refs[:chunks], refs[chunks:]
    dense_t, refs = refs[:slabs], refs[slabs:]
    dense1, refs = refs[:slabs], refs[slabs:]
    embed, done, refs = refs[0], refs[1], refs[2:]
    rewards, returns, refs = refs[0], refs[1], refs[2:]
    gfeats, refs = refs[:chunks], refs[chunks:]
    grads, deeper, second, predicted, g_pred, g_second, g_hidden, h1, h2 = (
        refs[:slabs],
        *refs[slabs:],
    )
    share = HID // slabs
    wide = dense1[0].shape[1] - 2 * share
    dense2 = [d[:, wide : wide + share] for d in dense1]
    dense3 = [d[:, wide + share : wide + 2 * share] for d in dense1]
    parts = [pl.ds(pl.multiple_of(ids[k] * share, 64), share) for k in range(slabs)]

    def through(weights, act, out):
        for k in range(slabs):
            out[parts[k], :] = dot_tn(weights[k], act)
        return out[...]

    def back(weights, grad, lanes):
        total = None
        for k in range(slabs):
            part = dot_nn(weights[k], grad[parts[k], lanes])
            total = part if total is None else total + part
        return total

    for c in range(chunks):
        lanes = slice(c * LANES, (c + 1) * LANES)
        hidden = None
        for k in range(slabs):
            part = dot_nn(dense1[k][:, :depth], feats[c][1, ids[k]])
            hidden = part if hidden is None else hidden + part
        act1, slope1 = silu_pair(hidden)
        act1 = act1.astype(BF)
        act2, slope2 = silu_pair(through(dense2, act1, second))
        act2 = act2.astype(BF)
        differ = through(dense3, act2, predicted) - embed[c]
        reward = jnp.sum(differ * differ, axis=0, keepdims=True) * (1.0 / HID)
        rewards[c] = reward
        returns[c] = discounted(reward, done[c])
        pred = differ.astype(BF)
        minus = (-differ).astype(BF)
        h1[:, lanes] = act1
        h2[:, lanes] = act2
        g_pred[:, lanes] = pred
        g_second[:, lanes] = (back(dense3, g_pred, lanes) * slope2).astype(BF)
        low = (back(dense2, g_second, lanes) * slope1).astype(BF)
        g_hidden[:, lanes] = low
        for k in range(slabs):
            gfeats[c][0, ids[k]] = dot_nn(dense_t[k][...], minus).astype(BF)
            gfeats[c][1, ids[k]] = dot_tn(dense1[k][:, :depth], low).astype(BF)
    deeper[:, :HID] = dot_nt(h1[...], g_second[...]).astype(BF)
    deeper[:, HID:] = dot_nt(h2[...], g_pred[...]).astype(BF)
    for k in range(slabs):
        both = jnp.concatenate([feats[c][1, ids[k]] for c in range(chunks)], axis=1)
        grads[k][...] = jnp.zeros_like(grads[k])
        grads[k][:, :depth] = dot_nt(g_hidden[...], both).astype(BF)


def heads(ids, feats, dense_t, dense1, embed, done):
    chunks, slabs = len(feats), len(dense1)
    depth = feats[0].shape[2]
    wide = dense1[0].shape[1] - 2 * (HID // slabs)
    full = lambda a: pl.BlockSpec(a.shape, lambda i, s: (0,) * len(a.shape))
    line = jax.ShapeDtypeStruct((chunks, 1, LANES), F32)
    outs = [
        line,
        line,
        *[jax.ShapeDtypeStruct(f.shape, BF) for f in feats],
        *[jax.ShapeDtypeStruct((HID, wide), BF)] * slabs,
        jax.ShapeDtypeStruct((HID, 2 * HID), BF),
    ]
    ins = [*feats, *dense_t, *dense1, embed, done]
    res = pl.pallas_call(
        functools.partial(heads_kernel, chunks, slabs, depth),
        grid_spec=pltpu.PrefetchScalarGridSpec(
            num_scalar_prefetch=1,
            grid=(1,),
            in_specs=[full(a) for a in ins],
            out_specs=[full(o) for o in outs],
            scratch_shapes=[pltpu.VMEM((HID, LANES), F32)] * 2
            + [pltpu.VMEM((HID, chunks * LANES), BF)] * 5,
        ),
        out_shape=outs,
        compiler_params=pltpu.CompilerParams(vmem_limit_bytes=VMEM_LIMIT),
        cost_estimate=cost(15),
        name="heads",
    )(ids, *ins)
    return res[0], res[1], res[2 : 2 + chunks], res[2 + chunks : -1], res[-1]


def edges_zero(ref, side, channels, top, bottom):
    line = side * channels
    ref[: top * line, :] = jnp.zeros((top * line, LANES), BF)
    ref[(side - bottom) * line :, :] = jnp.zeros((bottom * line, LANES), BF)
    for i in range(top, side - bottom):
        ref[i * line : i * line + top * channels, :] = jnp.zeros((top * channels, LANES), BF)
        ref[(i + 1) * line - bottom * channels : (i + 1) * line, :] = jnp.zeros(
            (bottom * channels, LANES), BF
        )


def deep_product(g, s3, d3p):
    for i in range(7):
        part = slice(i * 448, i * 448 + 448)
        d3p[((i + 2) * 11 + 2) * 64 : ((i + 2) * 11 + 9) * 64, :] = (
            g[part, :].astype(F32) * s3[part, :].astype(F32)
        ).astype(BF)


def deep_row(i, s2, v3, d3p, d2p):
    for b in range(3):
        window = stack([rows(d3p, ((i + r) * 11 + 3 * b) * 64, 320) for r in range(3)])
        up = dot_nn(v3[...], window)
        slope = rows(s2, (i * 9 + 3 * b) * 64, 192).astype(F32)
        put(d2p, ((i + 1) * 11 + 3 * b + 1) * 64, 192, (up * slope).astype(BF))


D1_LINE = 22 * C1
D1_ROWS = 22 * D1_LINE


def first_rows(m, s1, v2, d2p, d1):
    for n in range(10):
        window = stack([rows(d2p, ((m + a) * 11 + n) * 64, 128) for a in range(2)])
        slope = rows(s1, (m * 10 + n) * 128, 128, 128).astype(F32)
        grad = (dot_nn(v2[...], window) * slope).astype(BF)
        for dr in range(2):
            at = (2 * m + 1 + dr) * D1_LINE + (2 * n + 1) * C1
            put(d1, at, 64, grad[dr * 64 : dr * 64 + 64, :], 32)


def learner_kernel(g_in, s3_in, s2_in, s1_in, a2_in, a1_in, xs_in, v3, v2, s1hot, before, *refs):
    d1_out, grads = refs[-16:-14]
    g, s3, s2, s1, a2, a1, xs, d1, d3p, d2p, sum1, sum2, sum3, sems = refs[-14:]

    def move(source, target, index):
        return pltpu.make_async_copy(source, target, sems.at[index])

    def pair(v):
        return pl.ds(pl.multiple_of(v * 2 * A1_QROW, 256), 2 * A1_QROW)

    def line(v):
        return pl.ds(pl.multiple_of((4 * v + 1) * D1_LINE, 64), 4 * D1_LINE)

    move(g_in.at[1], g, 0).start()
    move(s3_in.at[1], s3, 1).start()
    move(s2_in.at[1], s2, 2).start()
    move(a2_in, a2, 3).start()
    edges_zero(d3p, 11, C3, 2, 2)
    edges_zero(d2p, 11, C2, 1, 1)
    edges_zero(d1, 22, C1, 1, 1)
    sum1[...] = jnp.zeros_like(sum1)
    sum2[...] = jnp.zeros_like(sum2)
    sum3[...] = jnp.zeros_like(sum3)
    move(g_in.at[1], g, 0).wait()
    move(s3_in.at[1], s3, 1).wait()
    for v in range(5):
        move(s1_in.at[1, pair(v)], s1.at[pair(v)], 6 + v).start()
        move(a1_in.at[pair(v)], a1.at[pair(v)], 11 + v).start()
        if v == 0:
            move(xs_in, xs, 4).start()
    deep_product(g, s3, d3p)
    move(s2_in.at[1], s2, 2).wait()
    move(a2_in, a2, 3).wait()

    @pl.loop(0, 4)
    def _(u):
        deep_row(2 * u, s2, v3, d3p, d2p)
        deep_row(2 * u + 1, s2, v3, d3p, d2p)
        left = jnp.concatenate(
            [
                stack([rows(d3p, ((2 * u + 2 + r) * 11 + 2 * b + 2) * 64, 128) for r in range(2)])
                for b in range(4)
            ],
            axis=1,
        )
        right = jnp.concatenate(
            [
                stack([rows(a2, ((2 * u + r) * 10 + 2 * b) * 64, 256) for r in range(4)])
                for b in range(4)
            ],
            axis=1,
        )
        sum3[...] += dot_nt(left, right)

    deep_row(8, s2, v3, d3p, d2p)
    move(xs_in, xs, 4).wait()

    @pl.loop(0, 5)
    def _(v):
        move(s1_in.at[1, pair(v)], s1.at[pair(v)], 6 + v).wait()
        move(a1_in.at[pair(v)], a1.at[pair(v)], 11 + v).wait()
        spots = [(2 * v + q, b) for q in range(2) for b in range(5)]
        first_rows(2 * v, s1, v2, d2p, d1)
        first_rows(2 * v + 1, s1, v2, d2p, d1)
        left = jnp.concatenate(
            [
                stack([rows(d2p, ((m + r) * 11 + 2 * b) * 64, 192) for r in range(2)])
                for m, b in spots
            ],
            axis=1,
        )
        right = jnp.concatenate(
            [rows(a1, m * A1_QROW + b * 256, 256, 256) for m, b in spots], axis=1
        )
        sum2[...] += dot_nt(left, right)
        left = jnp.concatenate(
            [
                stack(
                    [
                        rows(d1, (2 * m + 1 + dr) * D1_LINE + (4 * b + 1) * C1, 128, 32)
                        for dr in range(2)
                    ]
                )
                for m, b in spots
            ],
            axis=1,
        )
        right = jnp.concatenate(
            [
                stack([rows(xs, ((2 * m + r) * 21 + 4 * b) * 16, 80, 16) for r in range(3)])
                for m, b in spots
            ],
            axis=1,
        )
        sum1[...] += dot_nt(left, right)
        move(d1.at[line(v)], d1_out.at[line(v)], 5).start()

    for edge in (slice(0, D1_LINE), slice(21 * D1_LINE, D1_ROWS)):
        move(d1.at[edge], d1_out.at[edge], 5).start()

    grads[...] = before[...]
    total = jnp.zeros((64, 32), F32)
    for pos in range(8):
        block = sum1[pos * 32 : pos * 32 + 32, :]
        high = block.astype(BF)
        rest = block - high.astype(F32)
        mid = rest.astype(BF)
        low = (rest - mid.astype(F32)).astype(BF)
        r, c = divmod(pos, 4)
        hot = s1hot[(c // 2) * 4 + r * 2 + c % 2]
        total = total + (dot_nt(hot, high) + (dot_nt(hot, mid) + dot_nt(hot, low)))
    grads[576:640, 0:32] += total
    for rp in range(2):
        for qq in range(2):
            block = None
            for q in range(2):
                dj = q + 1 - qq
                at = ((1 - rp) * 3 + dj) * 64
                part = sum2[at : at + 64, q * 128 : q * 128 + 128]
                block = part if block is None else block + part
            block = block.T
            for d in range(4):
                tap = (2 * rp + d // 2) * 4 + 2 * qq + d % 2
                grads[tap * 32 : tap * 32 + 32, 64:128] += block[d * 32 : d * 32 + 32, :]
    for kr in range(3):
        block = None
        for pr in range(2):
            for pc in range(2):
                at = (pr * 2 + pc) * 64
                lane = (pr + kr) * 256 + pc * 64
                part = sum3[at : at + 64, lane : lane + 192]
                block = part if block is None else block + part
        grads[kr * 192 : kr * 192 + 192, 0:64] += block.T
    move(d1, d1_out, 5).wait()


PACKED = 768


def learner_backward(gfeat, s3, s2, s1, a2, a1, xs, v3, v2, before, deps=()):
    fixed = lambda s: pl.BlockSpec(s, lambda i: (0,) * len(s))
    learner = lambda a: pl.BlockSpec((None, *a.shape[1:]), lambda i: (1, 0, 0))
    s1hot = jnp.asarray(first_taps(), BF)
    return pl.pallas_call(
        learner_kernel,
        grid=(1,),
        in_specs=[pl.BlockSpec(memory_space=pl.ANY)] * 7
        + [learner(v3), learner(v2), fixed(s1hot.shape), fixed((PACKED, 128))]
        + waits(deps),
        out_specs=[pl.BlockSpec(memory_space=pl.ANY), fixed((PACKED, 128))],
        out_shape=[
            jax.ShapeDtypeStruct((D1_ROWS, LANES), BF),
            jax.ShapeDtypeStruct((PACKED, 128), F32),
        ],
        scratch_shapes=[
            pltpu.VMEM((r, LANES), BF)
            for r in (
                FEAT, FEAT, A2_ROWS, A1_ROWS, A2P_ROWS, A1_ROWS, PIX * PIX, D1_ROWS,
                PAD_ROWS, PAD_ROWS,
            )
        ]
        + [
            pltpu.VMEM((256, 240), F32),
            pltpu.VMEM((384, 256), F32),
            pltpu.VMEM((256, 1024), F32),
            pltpu.SemaphoreType.DMA((16,)),
        ],
        compiler_params=pltpu.CompilerParams(vmem_limit_bytes=VMEM_LIMIT),
        cost_estimate=cost(20),
        name="learner_backward",
    )(gfeat, s3, s2, s1, a2, a1, xs, v3, v2, s1hot, before, *deps)


def pixel_kernel(chunk, g_in, s3_in, s2_in, s1_in, d1_in, v3, v2, v1, perm, *refs):
    out_all = refs[-12]
    g, s3, s2, s1, mine, theirs, d3p, d2p, dxs, out, sems = refs[-11:]

    def move(source, target, index):
        return pltpu.make_async_copy(source, target, sems.at[index])

    def pair(v):
        return pl.ds(pl.multiple_of(v * 2 * A1_QROW, 256), 2 * A1_QROW)

    def line(v):
        return pl.ds(pl.multiple_of((4 * v + 1) * D1_LINE, 64), 4 * D1_LINE)

    def band(v):
        return pl.ds(pl.multiple_of(v * 4 * PATCH_ROWS, 64), 4 * PATCH_ROWS)

    here = pl.ds(chunk * GROUP, GROUP)

    move(g_in.at[0], g, 0).start()
    move(s3_in.at[0], s3, 1).start()
    move(s2_in.at[0], s2, 2).start()
    edges_zero(d3p, 11, C3, 2, 2)
    edges_zero(d2p, 11, C2, 1, 1)
    edges_zero(mine, 22, C1, 1, 1)
    theirs[:D1_LINE, :] = jnp.zeros((D1_LINE, LANES), BF)
    move(g_in.at[0], g, 0).wait()
    move(s3_in.at[0], s3, 1).wait()
    for v in range(5):
        move(s1_in.at[0, pair(v)], s1.at[pair(v)], 4 + v).start()
        move(d1_in.at[line(v)], theirs.at[line(v)], 9 + v).start()
    deep_product(g, s3, d3p)
    move(s2_in.at[0], s2, 2).wait()

    @pl.loop(0, 4)
    def _(u):
        deep_row(2 * u, s2, v3, d3p, d2p)
        deep_row(2 * u + 1, s2, v3, d3p, d2p)

    deep_row(8, s2, v3, d3p, d2p)

    def patches(v):
        for b in range(7):
            window = stack(
                [
                    rows(ref, (4 * v + r) * D1_LINE + 3 * b * C1, 128, 32)
                    for ref in (mine, theirs)
                    for r in range(5)
                ]
            )
            dx = dot_nn(v1[...], window).astype(BF)
            for pr in range(4):
                put(dxs, ((4 * v + pr) * 21 + 3 * b) * 16, 48, dx[pr * 48 : pr * 48 + 48], 16)

    def last_patches():
        w = jnp.concatenate([v1[:48, 0:128], v1[:48, 640:768]], axis=1)
        for b in range(7):
            at = slice(20 * D1_LINE + 3 * b * C1, 20 * D1_LINE + 3 * b * C1 + 128)
            window = stack([mine[at, :], theirs[at, :]])
            put(dxs, (20 * 21 + 3 * b) * 16, 48, dot_nn(w, window).astype(BF), 16)

    def turn(p):
        part = pl.ds(pl.multiple_of(p * PATCH_ROWS, 16), PATCH_ROWS)
        block = dot_tn(perm[...], dxs[part, :]).astype(BF)
        for e in range(GROUP):
            out[e, part, :] = block[:, e * STEPS : (e + 1) * STEPS]

    def first(v):
        first_rows(2 * v, s1, v2, d2p, mine)
        first_rows(2 * v + 1, s1, v2, d2p, mine)

    @pl.loop(0, 6)
    def _(v):
        @pl.when(v < 5)
        def _():
            move(s1_in.at[0, pair(v)], s1.at[pair(v)], 4 + v).wait()
            move(d1_in.at[line(v)], theirs.at[line(v)], 9 + v).wait()

        @pl.when(v == 0)
        def _():
            first(v)

        @pl.when(v == 1)
        def _():
            patches(v - 1)
            first(v)

        @pl.when((v >= 2) & (v < 5))
        def _():
            for k in range(4):
                turn(4 * (v - 2) + k)
            patches(v - 1)
            first(v)

        @pl.when(v == 5)
        def _():
            for k in range(4):
                turn(4 * (v - 2) + k)
            patches(v - 1)
            last_patches()

        @pl.when(v >= 2)
        def _():
            move(out.at[:, band(v - 2)], out_all.at[here, band(v - 2)], 3).start()

    for p in range(16, 21):
        turn(p)
    tail = pl.ds(16 * PATCH_ROWS, 5 * PATCH_ROWS)
    move(out.at[:, tail], out_all.at[here, tail], 3).start()
    move(out, out_all.at[here], 3).wait()


def pixel_backward(chunk, envs, gfeat, s3, s2, s1, d1, v3, v2, v1, perm, before, deps=()):
    fixed = lambda s: pl.BlockSpec(s, lambda i: (0,) * len(s))
    target = lambda a: pl.BlockSpec((None, *a.shape[1:]), lambda i: (0, 0, 0))
    ins = [gfeat, s3, s2, s1, d1, v3, v2, v1, perm]
    specs = [pl.BlockSpec(memory_space=pl.ANY)] * 5
    specs += [target(v3), target(v2), fixed(v1.shape), fixed(perm.shape)]
    aliases = {}
    if before is not None:
        aliases = {len(ins): 0}
        ins.append(before)
        specs.append(pl.BlockSpec(memory_space=pl.ANY))
    ins += deps
    specs += waits(deps)
    return pl.pallas_call(
        functools.partial(pixel_kernel, chunk),
        grid=(1,),
        in_specs=specs,
        out_specs=pl.BlockSpec(memory_space=pl.ANY),
        out_shape=jax.ShapeDtypeStruct((envs, PIX * PIX, STEPS), BF),
        scratch_shapes=[
            pltpu.VMEM((r, LANES), BF)
            for r in (
                FEAT, FEAT, A2_ROWS, A1_ROWS, D1_ROWS, D1_ROWS, PAD_ROWS, PAD_ROWS, PIX * PIX,
            )
        ]
        + [pltpu.VMEM((GROUP, PIX * PIX, STEPS), BF), pltpu.SemaphoreType.DMA((14,))],
        input_output_aliases=aliases,
        compiler_params=pltpu.CompilerParams(vmem_limit_bytes=VMEM_LIMIT),
        cost_estimate=cost(20),
        name="pixel_backward",
    )(*ins)


def whole(array):
    return pl.BlockSpec(array.shape, lambda *_: (0,) * len(array.shape))


def pack(index, dense1, dense2, dense3, wide, parts):
    lines, depth = dense1.shape
    share = HID // parts

    def kernel(at, one, two, three, out):
        out[...] = jnp.zeros_like(out)
        out[:, :depth] = one[...]
        for q in range(parts):

            @pl.when(at[0] == q)
            def _():
                out[:, wide : wide + share] = two[:, q * share : (q + 1) * share]
                out[:, wide + share :] = three[:, q * share : (q + 1) * share]

    result = jax.ShapeDtypeStruct((lines, wide + 2 * share), BF)
    return pl.pallas_call(
        kernel,
        grid_spec=pltpu.PrefetchScalarGridSpec(
            num_scalar_prefetch=1,
            grid=(1,),
            in_specs=[whole(dense1), whole(dense2), whole(dense3)],
            out_specs=whole(result),
        ),
        out_shape=result,
        cost_estimate=cost(1),
        name="pack",
    )(index, dense1, dense2, dense3)


def join(left, right, deps):
    count = len(left)

    def kernel(*refs):
        for k in range(count):
            total = refs[k][...].astype(F32) + refs[count + k][...].astype(F32)
            refs[-count + k][...] = total.astype(BF)

    lines, wide = left[0].shape
    block = pl.BlockSpec((lines // 4, wide), lambda i: (i, 0))
    return pl.pallas_call(
        kernel,
        grid=(4,),
        in_specs=[block] * (2 * count) + waits(deps),
        out_specs=[block] * count,
        out_shape=[jax.ShapeDtypeStruct((lines, wide), BF)] * count,
        cost_estimate=cost(2),
        name="join",
    )(*left, *right, *deps)


def split(arrays, index, groups, parts, deps):
    lines, wide = arrays[0].size // (arrays[0].shape[-1] * groups * parts), arrays[0].shape[-1]
    arrays = [a.reshape(groups, parts, lines, wide) for a in arrays]
    count = len(arrays)

    def kernel(at, *refs):
        for j in range(parts):
            source = lax.rem(at[0] + j, parts)
            total = refs[0][source].astype(F32)
            for k in range(1, count):
                total = total + refs[k][source].astype(F32)
            refs[-parts + j][...] = total.astype(BF)

    return pl.pallas_call(
        kernel,
        grid_spec=pltpu.PrefetchScalarGridSpec(
            num_scalar_prefetch=1,
            grid=(groups,),
            in_specs=[pl.BlockSpec((None, parts, lines, wide), lambda i, s: (i, 0, 0, 0))] * count
            + waits(deps),
            out_specs=[pl.BlockSpec((None, lines, wide), lambda i, s: (i, 0, 0))] * parts,
        ),
        out_shape=[jax.ShapeDtypeStruct((groups, lines, wide), BF)] * parts,
        cost_estimate=cost(2),
        name="split",
    )(index, *arrays, *deps)


def middle(blocks, depth, scale, deeper, small, deps):
    count = len(blocks)

    def kernel(*refs):
        total = refs[0][...].astype(F32)
        for k in range(1, count):
            total = total + refs[k][...].astype(F32)
        refs[-3][...] = total[:, :depth] * scale
        refs[-2][...] = refs[count][...]
        share = jnp.sum(refs[count + 1][...], axis=0) * scale
        refs[-1][...] = jnp.broadcast_to(share[None], refs[-1].shape)

    ins = [*blocks, deeper, small]
    outs = [
        jax.ShapeDtypeStruct((blocks[0].shape[0], depth), F32),
        jax.ShapeDtypeStruct(deeper.shape, deeper.dtype),
        jax.ShapeDtypeStruct(small.shape, small.dtype),
    ]
    return pl.pallas_call(
        kernel,
        grid=(1,),
        in_specs=[whole(a) for a in ins] + waits(deps),
        out_specs=[whole(a) for a in outs],
        out_shape=outs,
        cost_estimate=cost(2),
        name="middle",
    )(*ins, *deps)


def finish(deeper, scale, small, deps):
    count = len(deeper)

    def kernel(*refs):
        terms = [refs[k][...].astype(F32) for k in range(count)]
        while len(terms) > 1:
            joined = [a + b for a, b in zip(terms[::2], terms[1::2])]
            terms = joined + terms[len(joined) * 2 :]
        total = terms[0] * scale
        packed = refs[count]
        two, three, one, conv2, conv3 = refs[-5:]
        two[...] = total[:, :HID]
        three[...] = total[:, HID:]
        one[...] = packed[576:640, :C1]
        conv2[...] = packed[:512, 64:]
        conv3[...] = packed[:576, :64]

    ins = [*deeper, small]
    lines = deeper[0].shape[0]
    outs = [
        jax.ShapeDtypeStruct(s, F32)
        for s in ((lines, HID), (lines, HID), (64, C1), (512, C2), (576, C3))
    ]
    return pl.pallas_call(
        kernel,
        grid=(1,),
        in_specs=[whole(a) for a in ins] + waits(deps),
        out_specs=[whole(a) for a in outs],
        out_shape=outs,
        cost_estimate=cost(2),
        name="finish",
    )(*ins, *deps)


def shards(
    frames,
    episode_done,
    target_conv1,
    target_conv2,
    target_conv3,
    target_dense,
    predictor_conv1,
    predictor_conv2,
    predictor_conv3,
    predictor_dense1,
    predictor_dense2,
    predictor_dense3,
):
    everyone = ("dp", "mp")
    dp, mp = lax.axis_size("dp"), lax.axis_size("mp")
    envs_here = frames.shape[0]
    count = envs_here * STEPS
    chunks = count // LANES
    grad_scale = 1.0 / math.sqrt(count * dp * mp)
    cores = 2 if mp % 2 == 0 else 1
    chips = mp // cores
    pairs = 2 if dp % 2 == 0 else 1
    depth = target_dense.shape[0]
    wide = -(-depth // 128) * 128

    def from_chip(value, j):
        moves = [(i, ((i // cores + j) % chips) * cores + i % cores) for i in range(mp)]
        return lax.ppermute(value, "mp", moves)

    def other_core(value):
        return lax.ppermute(value, "mp", [(i, i ^ 1) for i in range(mp)])

    order = np.array(
        [
            [
                ((i // cores + chips - j) % chips) * cores + (i + k) % cores
                for k in range(cores)
                for j in range(chips)
            ]
            for i in range(mp)
        ],
        np.int32,
    )
    here = lax.axis_index("mp")
    place = lax.axis_index("dp")
    ids = lax.dynamic_index_in_dim(jnp.asarray(order), here, 0, keepdims=False)

    x = frames.swapaxes(1, 2)
    perm = jnp.asarray(patch_order(), BF)
    mine = pack(
        here.reshape(1), predictor_dense1.T, predictor_dense2, predictor_dense3, wide, mp
    )
    mine = lax.all_gather(mine, "dp", axis=0, tiled=True)
    dense_t = [target_dense] + [from_chip(target_dense, j) for j in range(1, chips)]
    w1, w2, w3a, w3b, v3, v2, v1 = make_weights(
        (target_conv1, target_conv2, target_conv3),
        (predictor_conv1, predictor_conv2, predictor_conv3),
    )
    saved = [forward(0, x, perm, w1, w2, w3a, w3b, [ids])]
    mine = after(mine, saved[0][5], *dense_t[1:])
    dense_t += [other_core(d) for d in dense_t] if cores == 2 else []
    dense1 = [mine] + [from_chip(mine, j) for j in range(1, chips)]
    for c in range(1, chunks):
        saved.append(forward(c, x, perm, w1, w2, w3a, w3b, [mine]))
    feats = [sv[5].reshape(2, mp, depth, LANES) for sv in saved]
    dense1[1:] = [after(d, saved[-1][5]) for d in dense1[1:]]
    embed, embeddings = embed_call(ids, feats, dense_t, dense1)
    dense1 += [other_core(d) for d in dense1] if cores == 2 else []
    rewards, returns, gfeats, grads, deeper = heads(
        ids, feats, dense_t, dense1, embed, episode_done.reshape(chunks, 1, LANES)
    )
    gfeats = [g.reshape(2, FEAT, LANES) for g in gfeats]

    deeper = lax.psum_scatter(deeper, "dp", scatter_dimension=0, tiled=True)
    kept = grads[:chips]
    if cores == 2:
        kept = join(kept, [other_core(g) for g in grads[chips:]], [])
    got = [from_chip(kept[j], chips - j) for j in range(1, chips)]
    small = jnp.zeros((PACKED, 128), F32)
    xs, a1, s1, a2, s2, feat, s3 = saved[0]
    first, small = learner_backward(gfeats[0], s3, s2, s1, a2, a1, xs, v3, v2, small, kept)
    first = [first]
    groups = dp // pairs
    total = split([kept[0], *got], (place % pairs).reshape(1), groups, pairs, [small])
    got = [
        lax.ppermute(total[j], "dp", [(i, i - i % pairs + (i + j) % pairs) for i in range(dp)])
        for j in range(1, pairs)
    ]
    for c in range(1, chunks):
        xs, a1, s1, a2, s2, feat, s3 = saved[c]
        grad, small = learner_backward(gfeats[c], s3, s2, s1, a2, a1, xs, v3, v2, small, total)
        first.append(grad)
    small = small.reshape(dp * mp, PACKED // (dp * mp), 128)
    spread = lax.all_to_all(small, everyone, split_axis=0, concat_axis=0, tiled=True)
    total = split([total[0], *got], (place // pairs).reshape(1), 1, groups, [small])
    total = [t.reshape(t.shape[1:]) for t in total]
    got = [
        lax.ppermute(total[j], "dp", [(i, (i + j * pairs) % dp) for i in range(dp)])
        for j in range(1, groups)
    ]

    xs, a1, s1, a2, s2, feat, s3 = saved[0]
    frame_grad = pixel_backward(
        0, envs_here, gfeats[0], s3, s2, s1, first[0], v3, v2, v1, perm, None, total
    )

    d1, deeper, share = middle([total[0], *got], depth, grad_scale, deeper, spread, [frame_grad])
    small = lax.all_to_all(share, everyone, split_axis=0, concat_axis=0, tiled=True)
    partner = (lambda i, j: i ^ j) if mp & (mp - 1) == 0 else (lambda i, j: (i + j) % mp)
    deeper = [deeper] + [
        lax.ppermute(deeper, "mp", [(i, partner(i, j)) for i in range(mp)]) for j in range(1, mp)
    ]
    for c in range(1, chunks):
        xs, a1, s1, a2, s2, feat, s3 = saved[c]
        frame_grad = pixel_backward(
            c, envs_here, gfeats[c], s3, s2, s1, first[c], v3, v2, v1, perm, frame_grad, [share]
        )
    d2, d3, e1, e2, e3 = finish(deeper, grad_scale, small.reshape(PACKED, 128), [frame_grad])
    return (
        embeddings.reshape(envs_here, STEPS, HID),
        rewards.reshape(envs_here, STEPS),
        returns.reshape(envs_here, STEPS),
        e1.reshape(8, 8, 1, C1),
        e2.reshape(4, 4, C1, C2),
        e3.reshape(3, 3, C2, C3),
        d1.T,
        d2,
        d3,
        frame_grad.swapaxes(1, 2),
    )


def solution(mesh):
    placed = (
        P(("dp", "mp"), None, None),
        P(("dp", "mp"), None),
        P(),
        P(),
        P(),
        P("mp", None),
        P(),
        P(),
        P(),
        P("mp", "dp"),
        P("dp", None),
        P("dp", None),
    )
    return jax.shard_map(
        shards,
        mesh=mesh,
        in_specs=placed,
        out_specs=(
            P(("dp", "mp"), None, None),
            P(("dp", "mp"), None),
            P(("dp", "mp"), None),
            P(),
            P(),
            P(),
            P("mp", "dp"),
            P("dp", None),
            P("dp", None),
            P(("dp", "mp"), None, None),
        ),
        check_vma=False,
    )
```

```python
import functools
import math

import jax
import jax.numpy as jnp
import numpy as np
from jax import lax
from jax.experimental import pallas as pl
from jax.experimental.pallas import tpu as pltpu
from jax.sharding import PartitionSpec as P

PIX = 84
HID = 512
STEPS = 128
FEAT = 3136
C1 = 32
C2 = 64
C3 = 64
GAMMA = 0.99
TRACE = 0.95

LANES = 256
GROUP = LANES // STEPS
PATCH_ROWS = 336
A1_ROWS = 12800
A1_QROW = 1280
A2_ROWS = 5184
A2P_ROWS = 6400
PAD_ROWS = 7744
BF = jnp.bfloat16
F32 = jnp.float32
VMEM_LIMIT = 60 * 1024 * 1024


def dot_nn(a, b):
    return lax.dot_general(a, b, (((1,), (0,)), ((), ())), preferred_element_type=F32)


def dot_nt(a, b):
    return lax.dot_general(a, b, (((1,), (1,)), ((), ())), preferred_element_type=F32)


def dot_tn(a, b):
    return lax.dot_general(a, b, (((0,), (0,)), ((), ())), preferred_element_type=F32)


def cost(us):
    return pl.CostEstimate(flops=int(us * 1e9), bytes_accessed=int(us * 1e6), transcendentals=0)


def whole(array):
    return pl.BlockSpec(array.shape, lambda *_: (0,) * len(array.shape))


def waits(others):
    return [pl.BlockSpec(memory_space=pl.ANY)] * len(others)


def after(value, *others):
    def kernel(*refs):
        del refs

    return pl.pallas_call(
        kernel,
        in_specs=waits((value, *others)),
        out_specs=pl.BlockSpec(memory_space=pl.ANY),
        out_shape=jax.ShapeDtypeStruct(value.shape, value.dtype),
        input_output_aliases={0: 0},
        cost_estimate=cost(0),
        name="after",
    )(value, *others)


def rows(ref, start, size, align=64):
    if not isinstance(start, int):
        start = pl.multiple_of(start, align)
    return ref[pl.ds(start, size), :]


def put(ref, start, size, value, align=64):
    if not isinstance(start, int):
        start = pl.multiple_of(start, align)
    ref[pl.ds(start, size), :] = value


def stack(parts):
    return jnp.concatenate(parts, axis=0)


def silu_half(h):
    turn = jnp.tanh(h)
    rise = 1.0 + turn
    act = h * rise
    return act, rise + act * (1.0 - turn)


def silu_pair(z):
    act, twice = silu_half(0.5 * z)
    return act, 0.5 * twice


def first_taps():
    out = np.zeros((8, 64, 240), np.float32)
    for q in range(2):
        for dr in range(2):
            for dc in range(2):
                r, c = dr, 2 * q + dc
                for kr in range(8):
                    for kc in range(8):
                        pr, u = divmod(4 * r + kr, 4)
                        pc, v = divmod(4 * c + kc, 4)
                        col = (pr * 5 + pc) * 16 + u * 4 + v
                        out[q * 4 + dr * 2 + dc, kr * 8 + kc, col] = 1.0
    return out


def patch_order():
    out = np.zeros((PATCH_ROWS, PATCH_ROWS), np.float32)
    for pc in range(21):
        for u in range(4):
            for v in range(4):
                out[pc * 16 + u * 4 + v, u * 84 + pc * 4 + v] = 1.0
    return out


def tap_order():
    out = np.zeros((64, 64), np.float32)
    for a in range(2):
        for b in range(2):
            for u in range(4):
                for v in range(4):
                    out[((a * 2 + b) * 4 + u) * 4 + v, (4 * a + u) * 8 + 4 * b + v] = 1.0
    return out


def place(width, block, count):
    out = np.zeros((block, count * width), np.float32)
    for j in range(count):
        for k in range(block):
            out[k, j * width + j * block + k] = 1.0
    return out


def weights_kernel(
    k1t, k2t, k3t, k1p, k2p, k3p, s1, tap, tile, half, quarter, w1, w2, w3a, w3b, v3, v2, v1
):
    for net, kernels in enumerate(((k1t, k2t, k3t), (k1p, k2p, k3p))):
        k1, k2, k3 = [(k[...].astype(F32) * 0.5).astype(BF) for k in kernels]
        one = k1
        for pos in range(8):
            w1[net, pos * 32 : pos * 32 + 32, :] = dot_tn(one, s1[pos]).astype(BF)
        w2[net, :, :] = jnp.zeros((192, 1024), BF)
        for rp in range(2):
            for qq in range(2):
                block = None
                for d in range(4):
                    kr, kc = 2 * rp + d // 2, 2 * qq + d % 2
                    part = dot_tn(
                        k2[(kr * 4 + kc) * 32 : (kr * 4 + kc) * 32 + 32, :],
                        quarter[:, d * 128 : d * 128 + 128],
                    )
                    block = part if block is None else block + part
                for p in range(3):
                    lane = rp * 512 + (p + qq) * 128
                    w2[net, p * 64 : p * 64 + 64, lane : lane + 128] = block.astype(BF)
        turned = [
            [dot_tn(k3[t * 64 : t * 64 + 64, :], half[:, s * 128 : s * 128 + 128]) for s in range(2)]
            for t in range(9)
        ]
        for out, group in ((w3a, 3), (w3b, 2)):
            wide = group + 2
            for p in range(group):
                for j in range((3 * wide + 1) // 2):
                    block = jnp.zeros((64, 128), F32)
                    for s in range(2):
                        k = 2 * j + s
                        r, c = divmod(k, wide)
                        if r < 3 and 0 <= c - p < 3:
                            block = block + turned[r * 3 + c - p][s]
                    lanes = min(128, 3 * wide * 64 - j * 128)
                    out[net, p * 64 : p * 64 + 64, j * 128 : j * 128 + lanes] = block[
                        :, :lanes
                    ].astype(BF)
        spread = dot_nn(k3, half[...])
        for p in range(3):
            for j in range(8):
                block = jnp.zeros((64, 128), F32)
                for s in range(2):
                    r, c = divmod(2 * j + s, 5)
                    kr, kc = 2 - r, p + 2 - c
                    if r < 3 and 0 <= kc < 3:
                        t = kr * 3 + kc
                        block = block + spread[t * 64 : t * 64 + 64, s * 128 : s * 128 + 128]
                lanes = min(128, 960 - j * 128)
                v3[net, p * 64 : p * 64 + 64, j * 128 : j * 128 + lanes] = block[:, :lanes].astype(BF)
        spread = dot_nn(k2, half[...])
        for d in range(4):
            dr, dc = divmod(d, 2)
            for a in range(2):
                block = jnp.zeros((32, 128), F32)
                for b in range(2):
                    t = (dr + 2 - 2 * a) * 4 + dc + 2 - 2 * b
                    block = block + spread[t * 32 : t * 32 + 32, b * 128 : b * 128 + 128]
                v2[net, d * 32 : d * 32 + 32, a * 128 : a * 128 + 128] = block.astype(BF)
        spread = dot_nn(dot_nn(tap[...], one).astype(BF), tile[...])
        lane = lax.broadcasted_iota(jnp.int32, (16, 128), 1) // 32
        for pr in range(4):
            for pc in range(3):
                for r in range(5):
                    block = jnp.zeros((16, 128), F32)
                    if 0 <= pr + 1 - r < 2:
                        for c in range(4):
                            if 0 <= pc + 1 - c < 2:
                                at = ((pr + 1 - r) * 2 + pc + 1 - c) * 16
                                block = jnp.where(lane == c, spread[at : at + 16, :], block)
                    first = (pr * 3 + pc) * 16
                    at = net * 640 + r * 128
                    v1[first : first + 16, at : at + 128] = block.astype(BF)


def make_weights(target, learner):
    s1 = jnp.asarray(first_taps(), BF)
    tap = jnp.asarray(tap_order(), BF)
    tile = jnp.asarray(np.tile(np.eye(32, dtype=np.float32), (1, 4)), BF)
    half = jnp.asarray(place(128, 64, 2), BF)
    quarter = jnp.asarray(place(128, 32, 4), BF)
    shapes = (
        (2, 256, 240),
        (2, 192, 1024),
        (2, 192, 960),
        (2, 128, 768),
        (2, 192, 960),
        (2, 128, 256),
        (192, 1280),
    )
    flat = []
    for k1, k2, k3 in (target, learner):
        flat += [k1.reshape(64, C1), k2.reshape(512, C2), k3.reshape(576, C3)]
    return pl.pallas_call(
        weights_kernel,
        out_shape=[jax.ShapeDtypeStruct(s, BF) for s in shapes],
        compiler_params=pltpu.CompilerParams(vmem_limit_bytes=VMEM_LIMIT),
        name="weights",
    )(*flat, s1, tap, tile, half, quarter)


KEPT = (A1_ROWS, A2_ROWS, FEAT, FEAT)
QUADS = ((0, 1), (2, 3), (4, 5), (6, 7), (8, 9))
SECONDS = ((0,), (1, 2), (3, 4), (5, 6), (7, 8))
THIRDS = ((), (0,), (1, 2), (3, 4), (5, 6))
PIECES = ((0, 5), (5, 9), (9, 13), (13, 17), (17, 21))


def forward_kernel(chunk, nets, arrange_here, pixels, perm, w1_in, w2_in, w3a_in, w3b_in, *refs):
    count = len(nets)
    refs = refs[len(refs) - (4 * count + 1 + 4 * count + 2 * count + 7) :]
    xs_out, refs = refs[0], refs[1:]
    outs, refs = [refs[4 * k : 4 * k + 4] for k in range(count)], refs[4 * count :]
    kept, refs = [refs[4 * k : 4 * k + 4] for k in range(count)], refs[4 * count :]
    acts, refs = [refs[2 * k : 2 * k + 2] for k in range(count)], refs[2 * count :]
    xs, x, w1, w2, w3a, w3b, sems = refs

    def move(source, into, index):
        return pltpu.make_async_copy(source, into, sems.at[index])

    def load(p):
        begin, end = PIECES[p]
        part = pl.ds(begin * PATCH_ROWS, (end - begin) * PATCH_ROWS)
        if arrange_here:
            return move(pixels.at[pl.ds(chunk * GROUP, GROUP), part], x.at[:, part], 9 + p)
        return move(pixels.at[part], xs.at[part], 9 + p)

    def arrange(p):
        if not arrange_here:
            return
        for k in range(*PIECES[p]):
            part = slice(k * PATCH_ROWS, (k + 1) * PATCH_ROWS)
            block = jnp.concatenate([x[e, part, :] for e in range(GROUP)], axis=1)
            xs[part, :] = dot_nn(perm[...], block).astype(BF)

    weights = [(w1_in, w1), (w2_in, w2), (w3a_in, w3a), (w3b_in, w3b)]
    load(0).start()
    move(*weights[0], 14).start()
    for p in range(1, 5):
        load(p).start()
    for k in range(1, 4):
        move(*weights[k], 14 + k).start()

    def leave(at, layer, half, start, size):
        act, twice = silu_half(half)
        value = half if nets[at] == 1 and layer < 2 else twice
        put(kept[at][(0, 1, 3)[layer]], start, size, value.astype(BF))
        return act.astype(BF)

    def first(at, quads):
        for m in quads:
            for b in range(5):
                window = stack([rows(xs, ((2 * m + r) * 21 + 4 * b) * 16, 80, 16) for r in range(3)])
                place = m * A1_QROW + b * 256
                act = leave(at, 0, dot_nn(w1[nets[at]], window), place, 256)
                put(acts[at][0], place, 256, act)

    def second(at, lines):
        for i in lines:
            for g in range(3):
                window = stack(
                    [rows(acts[at][0], ((i + r) * 10 + 3 * g) * 128, 512) for r in range(2)]
                )
                place = (i * 9 + 3 * g) * 64
                put(acts[at][1], place, 192, leave(at, 1, dot_nn(w2[nets[at]], window), place, 192))

    def third(at, lines):
        for i in lines:
            for c, group in ((0, 3), (3, 2), (5, 2)):
                window = stack(
                    [rows(acts[at][1], ((i + r) * 9 + c) * 64, (group + 2) * 64) for r in range(3)]
                )
                w = w3a if group == 3 else w3b
                place, size = (i * 7 + c) * 64, group * 64
                put(kept[at][2], place, size, leave(at, 2, dot_nn(w[nets[at]], window), place, size))

    def send(at, which, lines, line):
        part = pl.ds(lines[0] * line, len(lines) * line)
        move(kept[at][which].at[part], outs[at][which].at[part], 4 * at + which).start()

    steps = [(at, k) for at in range(count) for k in range(5)]
    load(0).wait()
    move(*weights[0], 14).wait()
    arrange(0)
    for t in range(len(steps) + 2):
        work = []
        if t + 1 < len(PIECES):
            load(t + 1).wait()
        if t == 1:
            for k in range(1, 4):
                move(*weights[k], 14 + k).wait()
        if t >= 2:
            at, k = steps[t - 2]
            if THIRDS[k]:
                third(at, THIRDS[k])
                work += [(at, 2, THIRDS[k], 448), (at, 3, THIRDS[k], 448)]
        if 1 <= t <= len(steps):
            at, k = steps[t - 1]
            second(at, SECONDS[k])
            work.append((at, 1, SECONDS[k], 576))
        if t < len(steps):
            at, k = steps[t]
            if t + 1 < len(PIECES):
                arrange(t + 1)
            first(at, QUADS[k])
            work.append((at, 0, QUADS[k], A1_QROW))
        for item in work:
            send(*item)
        if t == 4 and arrange_here:
            move(xs, xs_out, 8).start()
    for at in range(count):
        for which in range(4):
            move(kept[at][which], outs[at][which], 4 * at + which).wait()
    if arrange_here:
        move(xs, xs_out, 8).wait()


def forward(chunk, nets, pixels, perm, w1, w2, w3a, w3b, deps=()):
    arrange_here = pixels.ndim == 3
    ins = [w1, w2, w3a, w3b, *deps]
    outs = [jax.ShapeDtypeStruct((PIX * PIX if arrange_here else 16, LANES), BF)]
    outs += [jax.ShapeDtypeStruct((r, LANES), BF) for r in KEPT] * len(nets)
    res = pl.pallas_call(
        functools.partial(forward_kernel, chunk, nets, arrange_here),
        grid=(1,),
        in_specs=[pl.BlockSpec(memory_space=pl.ANY), whole(perm)] + waits(ins),
        out_specs=waits(outs),
        out_shape=outs,
        scratch_shapes=[pltpu.VMEM((r, LANES), BF) for r in KEPT * len(nets)]
        + [pltpu.VMEM((r, LANES), BF) for r in (A1_ROWS, A2_ROWS) * len(nets)]
        + [pltpu.VMEM((PIX * PIX, LANES), BF)]
        + [pltpu.VMEM((GROUP, PIX * PIX if arrange_here else 16, STEPS), BF)]
        + [pltpu.VMEM(w.shape, BF) for w in (w1, w2, w3a, w3b)]
        + [pltpu.SemaphoreType.DMA((18,))],
        compiler_params=pltpu.CompilerParams(vmem_limit_bytes=VMEM_LIMIT),
        cost_estimate=cost(12 * len(nets)),
        name="forward",
    )(pixels, perm, *ins)
    return res[0], [res[1 + 4 * k : 5 + 4 * k] for k in range(len(nets))]


def lanes_of(c):
    return pl.ds(c * LANES, LANES)


def embed_kernel(chunks, slabs, ids, *refs):
    feats, dense = refs[:chunks], refs[chunks : chunks + slabs]
    embed, embeddings, f, d, sems = refs[-5:]

    def feat(c, k):
        return pltpu.make_async_copy(
            feats[c].at[ids[k]], f.at[k, :, lanes_of(c)], sems.at[c, k]
        )

    def matrix(k):
        return pltpu.make_async_copy(dense[k], d.at[k], sems.at[chunks, k])

    for k in range(slabs):
        for c in range(chunks):
            feat(c, k).start()
        matrix(k).start()
    total = None
    for k in range(slabs):
        for c in range(chunks):
            feat(c, k).wait()
        matrix(k).wait()
        part = dot_tn(d[k], f[k])
        total = part if total is None else total + part
    embed[...] = total
    embeddings[...] = total.astype(BF).T


def embed_call(ids, feats, dense, deps=()):
    chunks, slabs = len(feats), len(dense)
    count = chunks * LANES
    outs = [jax.ShapeDtypeStruct((HID, count), F32), jax.ShapeDtypeStruct((count, HID), BF)]
    ins = [*feats, *dense, *deps]
    return pl.pallas_call(
        functools.partial(embed_kernel, chunks, slabs),
        grid_spec=pltpu.PrefetchScalarGridSpec(
            num_scalar_prefetch=1,
            grid=(1,),
            in_specs=waits(ins),
            out_specs=[whole(o) for o in outs],
            scratch_shapes=[
                pltpu.VMEM((slabs, feats[0].shape[1], count), BF),
                pltpu.VMEM((slabs, *dense[0].shape), BF),
                pltpu.SemaphoreType.DMA((chunks + 1, slabs)),
            ],
        ),
        out_shape=outs,
        compiler_params=pltpu.CompilerParams(vmem_limit_bytes=VMEM_LIMIT),
        cost_estimate=cost(5),
        name="embed",
    )(ids, *ins)


def discounted(rewards, done):
    carry = (GAMMA * TRACE) * (1.0 - done.astype(F32))
    step = lax.broadcasted_iota(jnp.int32, rewards.shape, 1) % STEPS
    carry = jnp.where(step == STEPS - 1, 0.0, carry)
    shift, count = 1, rewards.shape[1]
    while shift < STEPS:
        rewards = rewards + carry * pltpu.roll(rewards, count - shift, 1)
        carry = carry * pltpu.roll(carry, count - shift, 1)
        shift *= 2
    return rewards


def heads_kernel(chunks, slabs, depth, ids, *refs):
    feats, refs = refs[:chunks], refs[chunks:]
    dense_t, refs = refs[:slabs], refs[slabs:]
    dense1, refs = refs[:slabs], refs[slabs:]
    embed, done, rewards, returns, refs = *refs[:4], refs[4:]
    gfeats, refs = refs[:chunks], refs[chunks:]
    grads, refs = refs[:slabs], refs[slabs:]
    deeper, f, one, target, emb, gout, gone, gdeep, mid, sems, outs = refs
    share = HID // slabs
    wide = gone.shape[2]
    spots = [pl.ds(pl.multiple_of(ids[k] * share, 64), share) for k in range(slabs)]

    def move(source, into, at):
        return pltpu.make_async_copy(source, into, sems.at[at])

    def feat(c, k):
        return move(feats[c].at[ids[k]], f.at[k, :, lanes_of(c)], c * slabs + k)

    def matrix(k):
        return move(dense1[k], one.at[k], chunks * slabs + k)

    def other(k):
        return move(dense_t[k], target.at[k], (chunks + 1) * slabs + k)

    def result(c, net, k):
        return pltpu.make_async_copy(
            gout.at[net, k, :, lanes_of(c)], gfeats[c].at[net, ids[k]],
            outs.at[c * slabs + k, net],
        )

    def gradient(k):
        return pltpu.make_async_copy(gone.at[k], grads[k], outs.at[chunks * slabs + k, 0])

    late = pltpu.make_async_copy(gdeep, deeper, outs.at[chunks * slabs, 1])
    given = move(embed, emb, (chunks + 2) * slabs)

    for k in range(slabs):
        for c in range(chunks):
            feat(c, k).start()
        matrix(k).start()
    given.start()
    for k in range(slabs):
        other(k).start()

    hidden = None
    for k in range(slabs):
        for c in range(chunks):
            feat(c, k).wait()
        matrix(k).wait()
        part = dot_nn(one[k, :, :depth], f[k])
        hidden = part if hidden is None else hidden + part
    h1, slope1 = silu_pair(hidden)
    h1 = h1.astype(BF)
    for k in range(slabs):
        mid[spots[k], :] = dot_tn(one[k, :, wide : wide + share], h1)
    h2, slope2 = silu_pair(mid[...])
    h2 = h2.astype(BF)
    for k in range(slabs):
        mid[spots[k], :] = dot_tn(one[k, :, wide + share :], h2)
    given.wait()
    differ = mid[...] - emb[...]
    reward = jnp.sum(differ * differ, axis=0, keepdims=True) * (1.0 / HID)
    rewards[...] = reward
    returns[...] = discounted(reward, done[...])
    mid[...] = differ
    g_pred = differ.astype(BF)
    minus = (-differ).astype(BF)
    grad = None
    for k in range(slabs):
        part = dot_nn(one[k, :, wide + share :], mid[spots[k], :].astype(BF))
        grad = part if grad is None else grad + part
    grad = grad * slope2
    g_second = grad.astype(BF)
    mid[...] = grad
    grad = None
    for k in range(slabs):
        part = dot_nn(one[k, :, wide : wide + share], mid[spots[k], :].astype(BF))
        grad = part if grad is None else grad + part
    g_hidden = (grad * slope1).astype(BF)

    for k in range(slabs):
        if wide > depth:
            gone[k, :, depth:] = jnp.zeros((HID, wide - depth), BF)
        gone[k, :, :depth] = dot_nt(g_hidden, f[k]).astype(BF)
        gradient(k).start()
    gdeep[:, :HID] = dot_nt(h1, g_second).astype(BF)
    gdeep[:, HID:] = dot_nt(h2, g_pred).astype(BF)
    late.start()
    for k in range(slabs):
        gout[1, k] = dot_tn(one[k, :, :depth], g_hidden).astype(BF)
        for c in range(chunks):
            result(c, 1, k).start()
    for k in range(slabs):
        other(k).wait()
        gout[0, k] = dot_nn(target[k], minus).astype(BF)
        for c in range(chunks):
            result(c, 0, k).start()
    late.wait()
    for k in range(slabs):
        gradient(k).wait()
        for c in range(chunks):
            for net in range(2):
                result(c, net, k).wait()


def heads(ids, feats, dense_t, dense1, embed, done):
    chunks, slabs = len(feats), len(dense1)
    count = chunks * LANES
    depth = feats[0].shape[1]
    wide = dense1[0].shape[1] - 2 * (HID // slabs)
    line = jax.ShapeDtypeStruct((1, count), F32)
    outs = [
        line,
        line,
        *[jax.ShapeDtypeStruct((2, *f.shape), BF) for f in feats],
        *[jax.ShapeDtypeStruct((HID, wide), BF)] * slabs,
        jax.ShapeDtypeStruct((HID, 2 * HID), BF),
    ]
    ins = [*feats, *dense_t, *dense1, embed]
    res = pl.pallas_call(
        functools.partial(heads_kernel, chunks, slabs, depth),
        grid_spec=pltpu.PrefetchScalarGridSpec(
            num_scalar_prefetch=1,
            grid=(1,),
            in_specs=waits(ins) + [whole(done)],
            out_specs=[whole(line)] * 2 + waits(outs[2:]),
            scratch_shapes=[
                pltpu.VMEM((slabs, depth, count), BF),
                pltpu.VMEM((slabs, *dense1[0].shape), BF),
                pltpu.VMEM((slabs, *dense_t[0].shape), BF),
                pltpu.VMEM((HID, count), F32),
                pltpu.VMEM((2, slabs, depth, count), BF),
                pltpu.VMEM((slabs, HID, wide), BF),
                pltpu.VMEM((HID, 2 * HID), BF),
                pltpu.VMEM((HID, count), F32),
                pltpu.SemaphoreType.DMA(((chunks + 2) * slabs + 1,)),
                pltpu.SemaphoreType.DMA(((chunks + 1) * slabs, 2)),
            ],
        ),
        out_shape=outs,
        compiler_params=pltpu.CompilerParams(vmem_limit_bytes=VMEM_LIMIT),
        cost_estimate=cost(15),
        name="heads",
    )(ids, *ins, done)
    return res[0], res[1], res[2 : 2 + chunks], res[2 + chunks : -1], res[-1]


def edges_zero(ref, side, channels, top, bottom):
    line = side * channels
    spots = [(0, top * line), ((side - bottom) * line, bottom * line)]
    for i in range(top, side - bottom):
        spots += [(i * line, top * channels), ((i + 1) * line - bottom * channels, bottom * channels)]
    for start, size in spots:
        if size:
            ref[start : start + size, :] = jnp.zeros((size, LANES), BF)


def deep_product(i, g, s3, d3p):
    part = slice(i * 448, i * 448 + 448)
    d3p[((i + 2) * 11 + 2) * 64 : ((i + 2) * 11 + 9) * 64, :] = (
        g[part, :].astype(F32) * s3[part, :].astype(F32)
    ).astype(BF)


def deep_row(i, s2, v3, d3p, d2p, a2=None):
    for b in range(3):
        window = stack([rows(d3p, ((i + r) * 11 + 3 * b) * 64, 320) for r in range(3)])
        up = dot_nn(v3[...], window)
        slope = rows(s2, (i * 9 + 3 * b) * 64, 192).astype(F32)
        if a2 is not None:
            act, slope = silu_half(slope)
            put(a2, (i * 10 + 3 * b) * 64, 192, act.astype(BF))
        put(d2p, ((i + 1) * 11 + 3 * b + 1) * 64, 192, (up * slope).astype(BF))


D1_LINE = 22 * C1
D1_ROWS = 22 * D1_LINE


def first_rows(m, s1, v2, d2p, d1, a1=None):
    for n in range(10):
        window = stack([rows(d2p, ((m + a) * 11 + n) * 64, 128) for a in range(2)])
        slope = rows(s1, (m * 10 + n) * 128, 128, 128).astype(F32)
        if a1 is not None:
            act, slope = silu_half(slope)
            put(a1, (m * 10 + n) * 128, 128, act.astype(BF))
        grad = (dot_nn(v2[...], window) * slope).astype(BF)
        for dr in range(2):
            at = (2 * m + 1 + dr) * D1_LINE + (2 * n + 1) * C1
            put(d1, at, 64, grad[dr * 64 : dr * 64 + 64, :], 32)


def learner_kernel(add, g_in, s3_in, h2_in, h1_in, xs_in, v3, v2, s1hot, *refs):
    before = refs[0] if add else None
    d1_out, grads = refs[-16:-14]
    g, s3, h2, h1, a2, a1, xs, d1, d3p, d2p, sum1, sum2, sum3, sems = refs[-14:]

    def move(source, target, index):
        return pltpu.make_async_copy(source, target, sems.at[index])

    def pair(v):
        return pl.ds(v * 2 * A1_QROW, 2 * A1_QROW)

    def line(m):
        return pl.ds((2 * m + 1) * D1_LINE, 2 * D1_LINE)

    tops = [pl.ds(0, 4 * 448), pl.ds(4 * 448, 3 * 448)]

    middles = [pl.ds(0, 4 * 576), pl.ds(4 * 576, 5 * 576)]

    for k, part in enumerate(tops):
        move(g_in.at[1, part], g.at[part], 2 * k).start()
        move(s3_in.at[part], s3.at[part], 2 * k + 1).start()
        move(h2_in.at[middles[k]], h2.at[middles[k]], 4 + k).start()
        move(h1_in.at[pair(k)], h1.at[pair(k)], 6 + k).start()
    move(xs_in, xs, 12).start()
    for v in range(2, 5):
        move(h1_in.at[pair(v)], h1.at[pair(v)], 6 + v).start()
    edges_zero(d3p, 11, C3, 2, 2)
    edges_zero(d2p, 11, C2, 1, 1)
    edges_zero(d1, 22, C1, 1, 1)
    edges_zero(a2, 10, C2, 0, 1)
    sum1[...] = jnp.zeros_like(sum1)
    sum2[...] = jnp.zeros_like(sum2)
    sum3[...] = jnp.zeros_like(sum3)

    def wait_top(k):
        part = tops[k]
        move(g_in.at[1, part], g.at[part], 2 * k).wait()
        move(s3_in.at[part], s3.at[part], 2 * k + 1).wait()

    def conv3_terms(u):
        left = jnp.concatenate(
            [
                stack([rows(d3p, ((2 * u + 2 + r) * 11 + 2 * b + 2) * 64, 128) for r in range(2)])
                for b in range(4)
            ],
            axis=1,
        )
        right = jnp.concatenate(
            [
                stack([rows(a2, ((2 * u + r) * 10 + 2 * b) * 64, 256) for r in range(4)])
                for b in range(4)
            ],
            axis=1,
        )
        sum3[...] += dot_nt(left, right)

    def conv2_terms(m):
        left = jnp.concatenate(
            [
                stack([rows(d2p, ((m + r) * 11 + 2 * b) * 64, 192) for r in range(2)])
                for b in range(5)
            ],
            axis=1,
        )
        right = jnp.concatenate([rows(a1, m * A1_QROW + b * 256, 256) for b in range(5)], axis=1)
        sum2[...] += dot_nt(left, right)

    def conv1_terms(m):
        left = jnp.concatenate(
            [
                stack(
                    [
                        rows(d1, (2 * m + 1 + dr) * D1_LINE + (4 * b + 1) * C1, 128)
                        for dr in range(2)
                    ]
                )
                for b in range(5)
            ],
            axis=1,
        )
        right = jnp.concatenate(
            [
                stack([rows(xs, ((2 * m + r) * 21 + 4 * b) * 16, 80) for r in range(3)])
                for b in range(5)
            ],
            axis=1,
        )
        sum1[...] += dot_nt(left, right)

    def wait_pairs(*pairs):
        for v in pairs:
            move(h1_in.at[pair(v)], h1.at[pair(v)], 6 + v).wait()

    def send(*lines):
        for m in lines:
            move(d1.at[line(m)], d1_out.at[line(m)], 11).start()

    wait_top(0)
    for i in range(12):
        if i == 1:
            move(h2_in.at[middles[0]], h2.at[middles[0]], 4).wait()
        if i == 2:
            wait_pairs(0)
        if i == 4:
            wait_top(1)
            move(h2_in.at[middles[1]], h2.at[middles[1]], 5).wait()
            wait_pairs(1)
            move(xs_in, xs, 12).wait()
        if i == 6:
            wait_pairs(2)
            send(0, 1)
        if i == 8:
            wait_pairs(3, 4)
            send(2, 3)
        if i == 10:
            send(4, 5)
        if i < 7:
            deep_product(i, g, s3, d3p)
        if 1 <= i <= 9:
            deep_row(i - 1, h2, v3, d3p, d2p, a2)
        if i >= 3:
            conv2_terms(i - 3)
        if 2 <= i:
            first_rows(i - 2, h1, v2, d2p, d1, a1)
        if i >= 4:
            conv1_terms(i - 4)
        if i in (5, 7, 9, 10):
            conv3_terms((5, 7, 9, 10).index(i))
    send(6, 7, 8, 9)
    for edge in (slice(0, D1_LINE), slice(21 * D1_LINE, D1_ROWS)):
        move(d1.at[edge], d1_out.at[edge], 11).start()
    conv2_terms(9)
    conv1_terms(8)
    conv1_terms(9)

    grads[...] = jnp.zeros_like(grads) if before is None else before[...]
    total = jnp.zeros((64, 32), F32)
    for pos in range(8):
        block = sum1[pos * 32 : pos * 32 + 32, :]
        high = block.astype(BF)
        rest = block - high.astype(F32)
        mid = rest.astype(BF)
        low = (rest - mid.astype(F32)).astype(BF)
        r, c = divmod(pos, 4)
        hot = s1hot[(c // 2) * 4 + r * 2 + c % 2]
        total = total + (dot_nt(hot, high) + (dot_nt(hot, mid) + dot_nt(hot, low)))
    grads[576:640, 0:32] += total
    for rp in range(2):
        for qq in range(2):
            block = None
            for q in range(2):
                dj = q + 1 - qq
                at = ((1 - rp) * 3 + dj) * 64
                part = sum2[at : at + 64, q * 128 : q * 128 + 128]
                block = part if block is None else block + part
            block = block.T
            for d in range(4):
                tap = (2 * rp + d // 2) * 4 + 2 * qq + d % 2
                grads[tap * 32 : tap * 32 + 32, 64:128] += block[d * 32 : d * 32 + 32, :]
    for kr in range(3):
        block = None
        for pr in range(2):
            for pc in range(2):
                at = (pr * 2 + pc) * 64
                lane = (pr + kr) * 256 + pc * 64
                part = sum3[at : at + 64, lane : lane + 192]
                block = part if block is None else block + part
        grads[kr * 192 : kr * 192 + 192, 0:64] += block.T
    move(d1, d1_out, 11).wait()


PACKED = 768


def learner_backward(gfeat, s3, h2, h1, xs, v3, v2, before, deps=()):
    fixed = lambda s: pl.BlockSpec(s, lambda i: (0,) * len(s))
    learner = lambda a: pl.BlockSpec((None, *a.shape[1:]), lambda i: (1, 0, 0))
    s1hot = jnp.asarray(first_taps(), BF)
    before = [] if before is None else [before]
    return pl.pallas_call(
        functools.partial(learner_kernel, bool(before)),
        grid=(1,),
        in_specs=[pl.BlockSpec(memory_space=pl.ANY)] * 5
        + [learner(v3), learner(v2), fixed(s1hot.shape)]
        + [fixed((PACKED, 128))] * len(before)
        + waits(deps),
        out_specs=[pl.BlockSpec(memory_space=pl.ANY), fixed((PACKED, 128))],
        out_shape=[
            jax.ShapeDtypeStruct((D1_ROWS, LANES), BF),
            jax.ShapeDtypeStruct((PACKED, 128), F32),
        ],
        scratch_shapes=[
            pltpu.VMEM((r, LANES), BF)
            for r in (
                FEAT, FEAT, A2_ROWS, A1_ROWS, A2P_ROWS, A1_ROWS, PIX * PIX, D1_ROWS,
                PAD_ROWS, PAD_ROWS,
            )
        ]
        + [
            pltpu.VMEM((256, 240), F32),
            pltpu.VMEM((384, 256), F32),
            pltpu.VMEM((256, 1024), F32),
            pltpu.SemaphoreType.DMA((13,)),
        ],
        compiler_params=pltpu.CompilerParams(vmem_limit_bytes=VMEM_LIMIT),
        cost_estimate=cost(20),
        name="learner_backward",
    )(gfeat, s3, h2, h1, xs, v3, v2, s1hot, *before, *deps)


def pixel_kernel(chunk, g_in, s3_in, s2_in, s1_in, d1_in, v3, v2, v1, perm, *refs):
    out_all = refs[-12]
    g, s3, s2, s1, mine, theirs, d3p, d2p, dxs, out, sems = refs[-11:]

    def move(source, target, index):
        return pltpu.make_async_copy(source, target, sems.at[index])

    def pair(v):
        return pl.ds(v * 2 * A1_QROW, 2 * A1_QROW)

    def line(v):
        return pl.ds((4 * v + 1) * D1_LINE, 4 * D1_LINE)

    def band(v):
        return pl.ds(v * 4 * PATCH_ROWS, (4 if v < 4 else 5) * PATCH_ROWS)

    here = pl.ds(chunk * GROUP, GROUP)
    tops = [pl.ds(0, 4 * 448), pl.ds(4 * 448, 3 * 448)]

    middles = [pl.ds(0, 4 * 576), pl.ds(4 * 576, 5 * 576)]

    for k, part in enumerate(tops):
        move(g_in.at[0, part], g.at[part], 2 * k).start()
        move(s3_in.at[part], s3.at[part], 2 * k + 1).start()
        move(s2_in.at[middles[k]], s2.at[middles[k]], 14 + k).start()
        move(s1_in.at[pair(k)], s1.at[pair(k)], 4 + k).start()
        move(d1_in.at[line(k)], theirs.at[line(k)], 9 + k).start()
    edges_zero(d3p, 11, C3, 2, 2)
    edges_zero(d2p, 11, C2, 1, 1)
    edges_zero(mine, 22, C1, 1, 1)
    theirs[:D1_LINE, :] = jnp.zeros((D1_LINE, LANES), BF)

    def wait_top(k):
        part = tops[k]
        move(g_in.at[0, part], g.at[part], 2 * k).wait()
        move(s3_in.at[part], s3.at[part], 2 * k + 1).wait()

    def patches(v):
        for b in range(7):
            window = stack(
                [
                    rows(ref, (4 * v + r) * D1_LINE + 3 * b * C1, 128, 32)
                    for ref in (mine, theirs)
                    for r in range(5)
                ]
            )
            dx = dot_nn(v1[...], window).astype(BF)
            for pr in range(4):
                put(dxs, ((4 * v + pr) * 21 + 3 * b) * 16, 48, dx[pr * 48 : pr * 48 + 48], 16)

    def last_patches():
        w = jnp.concatenate([v1[:48, 0:128], v1[:48, 640:768]], axis=1)
        for b in range(7):
            at = slice(20 * D1_LINE + 3 * b * C1, 20 * D1_LINE + 3 * b * C1 + 128)
            window = stack([mine[at, :], theirs[at, :]])
            put(dxs, (20 * 21 + 3 * b) * 16, 48, dot_nn(w, window).astype(BF), 16)

    def turn(p):
        part = slice(p * PATCH_ROWS, (p + 1) * PATCH_ROWS)
        block = dot_tn(perm[...], dxs[part, :]).astype(BF)
        for e in range(GROUP):
            out[e, part, :] = block[:, e * STEPS : (e + 1) * STEPS]

    def wait_pairs(*pairs):
        for v in pairs:
            move(s1_in.at[pair(v)], s1.at[pair(v)], 4 + v).wait()
            move(d1_in.at[line(v)], theirs.at[line(v)], 9 + v).wait()

    for v in range(2, 5):
        move(s1_in.at[pair(v)], s1.at[pair(v)], 4 + v).start()
        move(d1_in.at[line(v)], theirs.at[line(v)], 9 + v).start()
    wait_top(0)
    for i in range(15):
        if i == 1:
            move(s2_in.at[middles[0]], s2.at[middles[0]], 14).wait()
        if i == 2:
            wait_pairs(0)
        if i == 4:
            wait_top(1)
            move(s2_in.at[middles[1]], s2.at[middles[1]], 15).wait()
            wait_pairs(1, 2)
        if i == 8:
            wait_pairs(3, 4)
        if i == 11:
            for v in (0, 1):
                move(out.at[:, band(v)], out_all.at[here, band(v)], 16).start()
        if i == 13:
            for v in (2, 3):
                move(out.at[:, band(v)], out_all.at[here, band(v)], 16).start()
        if i < 7:
            deep_product(i, g, s3, d3p)
        if i >= 6 and i % 2 == 0:
            v = (i - 6) // 2
            for p in range(4 * v, 4 * v + (4 if v < 4 else 5)):
                turn(p)
        if 1 <= i <= 9:
            deep_row(i - 1, s2, v3, d3p, d2p)
        if 4 <= i <= 12 and i % 2 == 0:
            v = (i - 4) // 2
            patches(v)
            if v == 4:
                last_patches()
        if 2 <= i <= 11:
            first_rows(i - 2, s1, v2, d2p, mine)
    move(out.at[:, band(4)], out_all.at[here, band(4)], 16).start()
    move(out, out_all.at[here], 16).wait()


def pixel_backward(chunk, envs, gfeat, s3, s2, s1, d1, v3, v2, v1, perm, before, deps=()):
    fixed = lambda s: pl.BlockSpec(s, lambda i: (0,) * len(s))
    target = lambda a: pl.BlockSpec((None, *a.shape[1:]), lambda i: (0, 0, 0))
    ins = [gfeat, s3, s2, s1, d1, v3, v2, v1, perm]
    specs = [pl.BlockSpec(memory_space=pl.ANY)] * 5
    specs += [target(v3), target(v2), fixed(v1.shape), fixed(perm.shape)]
    aliases = {}
    if before is not None:
        aliases = {len(ins): 0}
        ins.append(before)
        specs.append(pl.BlockSpec(memory_space=pl.ANY))
    ins += deps
    specs += waits(deps)
    return pl.pallas_call(
        functools.partial(pixel_kernel, chunk),
        grid=(1,),
        in_specs=specs,
        out_specs=pl.BlockSpec(memory_space=pl.ANY),
        out_shape=jax.ShapeDtypeStruct((envs, PIX * PIX, STEPS), BF),
        scratch_shapes=[
            pltpu.VMEM((r, LANES), BF)
            for r in (
                FEAT, FEAT, A2_ROWS, A1_ROWS, D1_ROWS, D1_ROWS, PAD_ROWS, PAD_ROWS, PIX * PIX,
            )
        ]
        + [pltpu.VMEM((GROUP, PIX * PIX, STEPS), BF), pltpu.SemaphoreType.DMA((17,))],
        input_output_aliases=aliases,
        compiler_params=pltpu.CompilerParams(vmem_limit_bytes=VMEM_LIMIT),
        cost_estimate=cost(20),
        name="pixel_backward",
    )(*ins)


def pack(index, dense1, dense2, dense3, wide, copies, parts, cores):
    lines, depth = dense1.shape
    share = HID // parts
    chips = parts // cores

    def kernel(at, one, two, three, out, ids):
        for k in range(cores):
            for j in range(chips):
                chip = lax.rem(at[0] // cores + chips - j, chips)
                ids[k * chips + j] = chip * cores + lax.rem(at[0] + k, cores)
        out[0] = jnp.zeros_like(out[0])
        out[0, :, :depth] = one[...]
        for q in range(parts):

            @pl.when(at[0] == q)
            def _():
                out[0, :, wide : wide + share] = two[:, q * share : (q + 1) * share]
                out[0, :, wide + share :] = three[:, q * share : (q + 1) * share]

        for k in range(1, copies):
            out[k] = out[0]

    result = jax.ShapeDtypeStruct((copies, lines, wide + 2 * share), BF)
    return pl.pallas_call(
        kernel,
        grid_spec=pltpu.PrefetchScalarGridSpec(
            num_scalar_prefetch=1,
            grid=(1,),
            in_specs=[whole(dense1), whole(dense2), whole(dense3)],
            out_specs=[whole(result), pl.BlockSpec(memory_space=pltpu.SMEM)],
        ),
        out_shape=[result, jax.ShapeDtypeStruct((parts,), jnp.int32)],
        cost_estimate=cost(1),
        name="pack",
    )(index, dense1, dense2, dense3)


def again(array):
    def kernel(source, out):
        out[...] = source[...]

    return pl.pallas_call(
        kernel,
        out_shape=jax.ShapeDtypeStruct(array.shape, array.dtype),
        cost_estimate=cost(1),
        name="again",
    )(array)


def join(left, right, deps):
    count = len(left)

    def kernel(*refs):
        for k in range(count):
            total = refs[k][...].astype(F32) + refs[count + k][...].astype(F32)
            refs[-count + k][...] = total.astype(BF)

    lines, wide = left[0].shape
    block = pl.BlockSpec((lines // 4, wide), lambda i: (i, 0))
    return pl.pallas_call(
        kernel,
        grid=(4,),
        in_specs=[block] * (2 * count) + waits(deps),
        out_specs=[block] * count,
        out_shape=[jax.ShapeDtypeStruct((lines, wide), BF)] * count,
        cost_estimate=cost(2),
        name="join",
    )(*left, *right, *deps)


def split(arrays, index, groups, parts, deps, terms=()):
    lines, wide = arrays[0].size // (arrays[0].shape[-1] * groups * parts), arrays[0].shape[-1]
    arrays = [a.reshape(groups, parts, lines, wide) for a in arrays]
    count = len(arrays)
    outs = [jax.ShapeDtypeStruct((groups, lines, wide), BF)] * parts
    outs += [jax.ShapeDtypeStruct(t.shape[1:], BF) for t in terms]
    results = len(outs)

    def kernel(at, *refs):
        for j in range(parts):
            source = lax.rem(at[0] + j, parts)
            for i in range(groups):
                total = refs[0][i, source].astype(F32)
                for k in range(1, count):
                    total = total + refs[k][i, source].astype(F32)
                refs[len(refs) - results + j][i] = total.astype(BF)
        for k in range(len(terms)):
            total = jnp.sum(refs[count + k][...].astype(F32), axis=0)
            refs[len(refs) - len(terms) + k][...] = total.astype(BF)

    return pl.pallas_call(
        kernel,
        grid_spec=pltpu.PrefetchScalarGridSpec(
            num_scalar_prefetch=1,
            grid=(1,),
            in_specs=[whole(a) for a in (*arrays, *terms)] + waits(deps),
            out_specs=[whole(o) for o in outs],
        ),
        out_shape=outs,
        cost_estimate=cost(2),
        name="split",
    )(index, *arrays, *terms, *deps)


def middle(blocks, depth, scale, small, deps):
    count = len(blocks)

    def kernel(*refs):
        total = refs[0][...].astype(F32)
        for k in range(1, count):
            total = total + refs[k][...].astype(F32)
        refs[-2][...] = total[:, :depth] * scale
        share = jnp.sum(refs[count][...], axis=0) * (0.5 * scale)
        refs[-1][...] = jnp.broadcast_to(share[None], refs[-1].shape)

    ins = [*blocks, small]
    outs = [
        jax.ShapeDtypeStruct((blocks[0].shape[0], depth), F32),
        jax.ShapeDtypeStruct(small.shape, small.dtype),
    ]
    return pl.pallas_call(
        kernel,
        grid=(1,),
        in_specs=[whole(a) for a in ins] + waits(deps),
        out_specs=[whole(a) for a in outs],
        out_shape=outs,
        cost_estimate=cost(2),
        name="middle",
    )(*ins, *deps)


def finish(deeper, scale, small, deps):
    count = len(deeper)

    def kernel(*refs):
        terms = [refs[k][...].astype(F32) for k in range(count)]
        while len(terms) > 1:
            joined = [a + b for a, b in zip(terms[::2], terms[1::2])]
            terms = joined + terms[len(joined) * 2 :]
        total = terms[0] * scale
        packed = refs[count]
        two, three, one, conv2, conv3 = refs[-5:]
        two[...] = total[:, :HID]
        three[...] = total[:, HID:]
        one[...] = packed[576:640, :C1]
        conv2[...] = packed[:512, 64:]
        conv3[...] = packed[:576, :64]

    ins = [*deeper, small]
    lines = deeper[0].shape[0]
    outs = [
        jax.ShapeDtypeStruct(s, F32)
        for s in ((lines, HID), (lines, HID), (64, C1), (512, C2), (576, C3))
    ]
    return pl.pallas_call(
        kernel,
        grid=(1,),
        in_specs=[whole(a) for a in ins] + waits(deps),
        out_specs=[whole(a) for a in outs],
        out_shape=outs,
        cost_estimate=cost(2),
        name="finish",
    )(*ins, *deps)


def shards(
    frames,
    episode_done,
    target_conv1,
    target_conv2,
    target_conv3,
    target_dense,
    predictor_conv1,
    predictor_conv2,
    predictor_conv3,
    predictor_dense1,
    predictor_dense2,
    predictor_dense3,
):
    everyone = ("dp", "mp")
    dp, mp = lax.axis_size("dp"), lax.axis_size("mp")
    envs_here = frames.shape[0]
    count = envs_here * STEPS
    chunks = count // LANES
    grad_scale = 1.0 / math.sqrt(count * dp * mp)
    cores = 2 if mp % 2 == 0 else 1
    chips = mp // cores
    pairs = 2 if dp % 2 == 0 else 1
    depth = target_dense.shape[0]
    wide = -(-depth // 128) * 128

    def from_chip(value, j):
        moves = [(i, ((i // cores + j) % chips) * cores + i % cores) for i in range(mp)]
        return lax.ppermute(value, "mp", moves)

    def other_core(value):
        return lax.ppermute(value, "mp", [(i, i ^ 1) for i in range(mp)])

    here = lax.axis_index("mp")
    place = lax.axis_index("dp")

    x = frames.swapaxes(1, 2)
    perm = jnp.asarray(patch_order(), BF)
    mine, ids = pack(
        here.reshape(1), predictor_dense1.T, predictor_dense2, predictor_dense3, wide, dp, mp, cores
    )
    mine = lax.all_to_all(mine, "dp", split_axis=0, concat_axis=0, tiled=True)
    mine = mine.reshape(HID, mine.shape[2])
    source = again(target_dense)
    dense_t = [target_dense] + [from_chip(source, j) for j in range(1, chips)]
    w1, w2, w3a, w3b, v3, v2, v1 = make_weights(
        (target_conv1, target_conv2, target_conv3),
        (predictor_conv1, predictor_conv2, predictor_conv3),
    )
    fixed = (perm, w1, w2, w3a, w3b)
    xs, (learner, target) = forward(0, (1, 0), x, *fixed)
    saved = [(xs, learner, target)]
    mine = after(mine, target[2], *dense_t[1:])
    dense_t += [other_core(d) for d in dense_t] if cores == 2 else []
    dense1 = [mine] + [from_chip(mine, j) for j in range(1, chips)]
    for c in range(1, chunks):
        xs, (learner, target) = forward(c, (1, 0), x, *fixed, [mine])
        saved.append((xs, learner, target))
    feats = [[sv[k][2].reshape(mp, depth, LANES) for sv in saved] for k in (2, 1)]
    embed, embeddings = embed_call(ids, feats[0], dense_t)
    dense1[1:] = [after(d, embed) for d in dense1[1:]]
    dense1 += [other_core(d) for d in dense1] if cores == 2 else []
    rewards, returns, gfeats, grads, deeper = heads(
        ids, feats[1], dense_t, dense1, embed, episode_done.reshape(1, count)
    )
    gfeats = [g.reshape(2, FEAT, LANES) for g in gfeats]

    deeper = deeper.reshape(dp, HID // dp, 2 * HID)
    deeper = lax.all_to_all(deeper, "dp", split_axis=0, concat_axis=0, tiled=True)
    kept = grads[:chips]
    terms = [kept[0]]
    if cores == 2:
        got = [other_core(g) for g in grads[chips:][::-1]][::-1]
        terms.append(got[0])
        kept = [kept[0]] + (list(join(kept[1:], got[1:], [])) if chips > 1 else [])
    terms += [from_chip(kept[j], chips - j) for j in range(1, chips)]
    def learner_part(c, small, deps):
        xs, (h1, h2, _, s3), _ = saved[c]
        return learner_backward(gfeats[c], s3, h2, h1, xs, v3, v2, small, deps)

    def pixel_part(c, frame_grad, deps):
        s1, s2, _, s3 = saved[c][2]
        return pixel_backward(
            c, envs_here, gfeats[c], s3, s2, s1, first[c], v3, v2, v1, perm, frame_grad, deps
        )

    first, small = learner_part(0, None, kept[1:])
    first = [first]
    groups = dp // pairs
    total = split(terms, (place % pairs).reshape(1), groups, pairs, [small])
    got = [
        lax.ppermute(total[j], "dp", [(i, i - i % pairs + (i + j) % pairs) for i in range(dp)])
        for j in range(1, pairs)
    ]
    for c in range(1, chunks):
        grad, small = learner_part(c, small, total)
        first.append(grad)
    small = small.reshape(dp * mp, PACKED // (dp * mp), 128)
    spread = lax.all_to_all(small, everyone, split_axis=0, concat_axis=0, tiled=True)
    *total, deeper = split(
        [total[0], *got], (place // pairs).reshape(1), 1, groups, [small], [deeper]
    )
    total = [t.reshape(t.shape[1:]) for t in total]
    got = [
        lax.ppermute(total[j], "dp", [(i, (i + j * pairs) % dp) for i in range(dp)])
        for j in range(1, groups)
    ]

    partner = (lambda i, j: i ^ j) if mp & (mp - 1) == 0 else (lambda i, j: (i + j) % mp)
    deeper = [deeper] + [
        lax.ppermute(deeper, "mp", [(i, partner(i, j)) for i in range(mp)]) for j in range(1, mp)
    ]

    frame_grad = pixel_part(0, None, total)
    d1, share = middle([total[0], *got], depth, grad_scale, spread, [frame_grad])
    small = lax.all_to_all(share, everyone, split_axis=0, concat_axis=0, tiled=True)
    for c in range(1, chunks):
        frame_grad = pixel_part(c, frame_grad, [share])
    d2, d3, e1, e2, e3 = finish(deeper, grad_scale, small.reshape(PACKED, 128), [frame_grad])
    return (
        embeddings.reshape(envs_here, STEPS, HID),
        rewards.reshape(envs_here, STEPS),
        returns.reshape(envs_here, STEPS),
        e1.reshape(8, 8, 1, C1),
        e2.reshape(4, 4, C1, C2),
        e3.reshape(3, 3, C2, C3),
        d1.T,
        d2,
        d3,
        frame_grad.swapaxes(1, 2),
    )


def solution(mesh):
    placed = (
        P(("dp", "mp"), None, None),
        P(("dp", "mp"), None),
        P(),
        P(),
        P(),
        P("mp", None),
        P(),
        P(),
        P(),
        P("mp", "dp"),
        P("dp", None),
        P("dp", None),
    )
    return jax.shard_map(
        shards,
        mesh=mesh,
        in_specs=placed,
        out_specs=(
            P(("dp", "mp"), None, None),
            P(("dp", "mp"), None),
            P(("dp", "mp"), None),
            P(),
            P(),
            P(),
            P("mp", "dp"),
            P("dp", None),
            P("dp", None),
            P(("dp", "mp"), None, None),
        ),
        check_vma=False,
    )
```

```python
import functools
import math

import jax
import jax.numpy as jnp
import numpy as np
from jax import lax
from jax.experimental import pallas as pl
from jax.experimental.pallas import tpu as pltpu
from jax.sharding import PartitionSpec as P

PIX = 84
HID = 512
STEPS = 128
FEAT = 3136
C1 = 32
C2 = 64
C3 = 64
GAMMA = 0.99
TRACE = 0.95

LANES = 256
GROUP = LANES // STEPS
PATCH_ROWS = 336
A1_ROWS = 12800
A1_QROW = 1280
A2_ROWS = 5184
A2P_ROWS = 6400
PAD_ROWS = 7744
BF = jnp.bfloat16
F32 = jnp.float32
VMEM_LIMIT = int(63.5 * 1024 * 1024)


def dot_nn(a, b):
    return lax.dot_general(a, b, (((1,), (0,)), ((), ())), preferred_element_type=F32)


def dot_nt(a, b):
    return lax.dot_general(a, b, (((1,), (1,)), ((), ())), preferred_element_type=F32)


def dot_tn(a, b):
    return lax.dot_general(a, b, (((0,), (0,)), ((), ())), preferred_element_type=F32)


def cost(us):
    return pl.CostEstimate(flops=int(us * 1e9), bytes_accessed=int(us * 1e6), transcendentals=0)


def whole(array):
    return pl.BlockSpec(array.shape, lambda *_: (0,) * len(array.shape))


def waits(others):
    return [pl.BlockSpec(memory_space=pl.ANY)] * len(others)


def after(value, *others):
    def kernel(*refs):
        del refs

    return pl.pallas_call(
        kernel,
        in_specs=waits((value, *others)),
        out_specs=pl.BlockSpec(memory_space=pl.ANY),
        out_shape=jax.ShapeDtypeStruct(value.shape, value.dtype),
        input_output_aliases={0: 0},
        cost_estimate=cost(0),
        name="after",
    )(value, *others)


def rows(ref, start, size, align=64):
    if not isinstance(start, int):
        start = pl.multiple_of(start, align)
    return ref[pl.ds(start, size), :]


def put(ref, start, size, value, align=64):
    if not isinstance(start, int):
        start = pl.multiple_of(start, align)
    ref[pl.ds(start, size), :] = value


def stack(parts):
    return jnp.concatenate(parts, axis=0)


def silu_half(h):
    turn = jnp.tanh(h)
    rise = 1.0 + turn
    act = h * rise
    return act, rise + act * (1.0 - turn)


def silu_pair(z):
    act, twice = silu_half(0.5 * z)
    return act, 0.5 * twice


def first_taps():
    out = np.zeros((8, 64, 240), np.float32)
    for q in range(2):
        for dr in range(2):
            for dc in range(2):
                r, c = dr, 2 * q + dc
                for kr in range(8):
                    for kc in range(8):
                        pr, u = divmod(4 * r + kr, 4)
                        pc, v = divmod(4 * c + kc, 4)
                        col = (pr * 5 + pc) * 16 + u * 4 + v
                        out[q * 4 + dr * 2 + dc, kr * 8 + kc, col] = 1.0
    return out


def patch_order():
    out = np.zeros((PATCH_ROWS, PATCH_ROWS), np.float32)
    for pc in range(21):
        for u in range(4):
            for v in range(4):
                out[pc * 16 + u * 4 + v, u * 84 + pc * 4 + v] = 1.0
    return out


def tap_order():
    out = np.zeros((64, 64), np.float32)
    for a in range(2):
        for b in range(2):
            for u in range(4):
                for v in range(4):
                    out[((a * 2 + b) * 4 + u) * 4 + v, (4 * a + u) * 8 + 4 * b + v] = 1.0
    return out


def place(width, block, count):
    out = np.zeros((block, count * width), np.float32)
    for j in range(count):
        for k in range(block):
            out[k, j * width + j * block + k] = 1.0
    return out


def weights_kernel(
    k1t, k2t, k3t, k1p, k2p, k3p, s1, tap, tile, half, quarter, w1, w2, w3a, w3b, v3, v2, v1
):
    for net, kernels in enumerate(((k1t, k2t, k3t), (k1p, k2p, k3p))):
        k1, k2, k3 = [(k[...].astype(F32) * 0.5).astype(BF) for k in kernels]
        one = k1
        for pos in range(8):
            w1[net, pos * 32 : pos * 32 + 32, :] = dot_tn(one, s1[pos]).astype(BF)
        w2[net, :, :] = jnp.zeros((192, 1024), BF)
        for rp in range(2):
            for qq in range(2):
                block = None
                for d in range(4):
                    kr, kc = 2 * rp + d // 2, 2 * qq + d % 2
                    part = dot_tn(
                        k2[(kr * 4 + kc) * 32 : (kr * 4 + kc) * 32 + 32, :],
                        quarter[:, d * 128 : d * 128 + 128],
                    )
                    block = part if block is None else block + part
                for p in range(3):
                    lane = rp * 512 + (p + qq) * 128
                    w2[net, p * 64 : p * 64 + 64, lane : lane + 128] = block.astype(BF)
        turned = [
            [dot_tn(k3[t * 64 : t * 64 + 64, :], half[:, s * 128 : s * 128 + 128]) for s in range(2)]
            for t in range(9)
        ]
        for out, group in ((w3a, 3), (w3b, 2)):
            wide = group + 2
            for p in range(group):
                for j in range((3 * wide + 1) // 2):
                    block = jnp.zeros((64, 128), F32)
                    for s in range(2):
                        k = 2 * j + s
                        r, c = divmod(k, wide)
                        if r < 3 and 0 <= c - p < 3:
                            block = block + turned[r * 3 + c - p][s]
                    lanes = min(128, 3 * wide * 64 - j * 128)
                    out[net, p * 64 : p * 64 + 64, j * 128 : j * 128 + lanes] = block[
                        :, :lanes
                    ].astype(BF)
        spread = dot_nn(k3, half[...])
        for p in range(3):
            for j in range(8):
                block = jnp.zeros((64, 128), F32)
                for s in range(2):
                    r, c = divmod(2 * j + s, 5)
                    kr, kc = 2 - r, p + 2 - c
                    if r < 3 and 0 <= kc < 3:
                        t = kr * 3 + kc
                        block = block + spread[t * 64 : t * 64 + 64, s * 128 : s * 128 + 128]
                lanes = min(128, 960 - j * 128)
                v3[net, p * 64 : p * 64 + 64, j * 128 : j * 128 + lanes] = block[:, :lanes].astype(BF)
        spread = dot_nn(k2, half[...])
        for d in range(4):
            dr, dc = divmod(d, 2)
            for a in range(2):
                block = jnp.zeros((32, 128), F32)
                for b in range(2):
                    t = (dr + 2 - 2 * a) * 4 + dc + 2 - 2 * b
                    block = block + spread[t * 32 : t * 32 + 32, b * 128 : b * 128 + 128]
                v2[net, d * 32 : d * 32 + 32, a * 128 : a * 128 + 128] = block.astype(BF)
        spread = dot_nn(dot_nn(tap[...], one).astype(BF), tile[...])
        lane = lax.broadcasted_iota(jnp.int32, (16, 128), 1) // 32
        for pr in range(4):
            for pc in range(3):
                for r in range(5):
                    block = jnp.zeros((16, 128), F32)
                    if 0 <= pr + 1 - r < 2:
                        for c in range(4):
                            if 0 <= pc + 1 - c < 2:
                                at = ((pr + 1 - r) * 2 + pc + 1 - c) * 16
                                block = jnp.where(lane == c, spread[at : at + 16, :], block)
                    first = (pr * 3 + pc) * 16
                    at = net * 640 + r * 128
                    v1[first : first + 16, at : at + 128] = block.astype(BF)


def make_weights(target, learner):
    s1 = jnp.asarray(first_taps(), BF)
    tap = jnp.asarray(tap_order(), BF)
    tile = jnp.asarray(np.tile(np.eye(32, dtype=np.float32), (1, 4)), BF)
    half = jnp.asarray(place(128, 64, 2), BF)
    quarter = jnp.asarray(place(128, 32, 4), BF)
    shapes = (
        (2, 256, 240),
        (2, 192, 1024),
        (2, 192, 960),
        (2, 128, 768),
        (2, 192, 960),
        (2, 128, 256),
        (192, 1280),
    )
    flat = []
    for k1, k2, k3 in (target, learner):
        flat += [k1.reshape(64, C1), k2.reshape(512, C2), k3.reshape(576, C3)]
    return pl.pallas_call(
        weights_kernel,
        out_shape=[jax.ShapeDtypeStruct(s, BF) for s in shapes],
        compiler_params=pltpu.CompilerParams(vmem_limit_bytes=VMEM_LIMIT),
        name="weights",
    )(*flat, s1, tap, tile, half, quarter)


KEPT = (A1_ROWS, A2_ROWS, FEAT, FEAT)
QUADS = ((0, 1), (2, 3), (4, 5), (6, 7), (8, 9))
SECONDS = ((0,), (1, 2), (3, 4), (5, 6), (7, 8))
THIRDS = ((), (0,), (1, 2), (3, 4), (5, 6))
PIECES = ((0, 5), (5, 9), (9, 13), (13, 17), (17, 21))


def forward_kernel(chunk, nets, arrange_here, pixels, perm, w1_in, w2_in, w3a_in, w3b_in, *refs):
    count = len(nets)
    refs = refs[len(refs) - (4 * count + 1 + 4 * count + 2 * count + 7) :]
    xs_out, refs = refs[0], refs[1:]
    outs, refs = [refs[4 * k : 4 * k + 4] for k in range(count)], refs[4 * count :]
    kept, refs = [refs[4 * k : 4 * k + 4] for k in range(count)], refs[4 * count :]
    acts, refs = [refs[2 * k : 2 * k + 2] for k in range(count)], refs[2 * count :]
    xs, x, w1, w2, w3a, w3b, sems = refs

    def move(source, into, index):
        return pltpu.make_async_copy(source, into, sems.at[index])

    def load(p):
        begin, end = PIECES[p]
        part = pl.ds(begin * PATCH_ROWS, (end - begin) * PATCH_ROWS)
        if arrange_here:
            return move(pixels.at[pl.ds(chunk * GROUP, GROUP), part], x.at[:, part], 9 + p)
        return move(pixels.at[part], xs.at[part], 9 + p)

    def arrange(p):
        if not arrange_here:
            return
        for k in range(*PIECES[p]):
            part = slice(k * PATCH_ROWS, (k + 1) * PATCH_ROWS)
            block = jnp.concatenate([x[e, part, :] for e in range(GROUP)], axis=1)
            xs[part, :] = dot_nn(perm[...], block).astype(BF)

    weights = [(w1_in, w1), (w2_in, w2), (w3a_in, w3a), (w3b_in, w3b)]
    load(0).start()
    move(*weights[0], 14).start()
    for p in range(1, 5):
        load(p).start()
    for k in range(1, 4):
        move(*weights[k], 14 + k).start()

    def leave(at, layer, half, start, size):
        act, twice = silu_half(half)
        value = half if nets[at] == 1 and layer < 2 else twice
        put(kept[at][(0, 1, 3)[layer]], start, size, value.astype(BF))
        return act.astype(BF)

    def first(at, quads):
        for m in quads:
            for b in range(5):
                window = stack([rows(xs, ((2 * m + r) * 21 + 4 * b) * 16, 80, 16) for r in range(3)])
                place = m * A1_QROW + b * 256
                act = leave(at, 0, dot_nn(w1[nets[at]], window), place, 256)
                put(acts[at][0], place, 256, act)

    def second(at, lines):
        for i in lines:
            for g in range(3):
                window = stack(
                    [rows(acts[at][0], ((i + r) * 10 + 3 * g) * 128, 512) for r in range(2)]
                )
                place = (i * 9 + 3 * g) * 64
                put(acts[at][1], place, 192, leave(at, 1, dot_nn(w2[nets[at]], window), place, 192))

    def third(at, lines):
        for i in lines:
            for c, group in ((0, 3), (3, 2), (5, 2)):
                window = stack(
                    [rows(acts[at][1], ((i + r) * 9 + c) * 64, (group + 2) * 64) for r in range(3)]
                )
                w = w3a if group == 3 else w3b
                place, size = (i * 7 + c) * 64, group * 64
                put(kept[at][2], place, size, leave(at, 2, dot_nn(w[nets[at]], window), place, size))

    def send(at, which, lines, line):
        part = pl.ds(lines[0] * line, len(lines) * line)
        move(kept[at][which].at[part], outs[at][which].at[part], 4 * at + which).start()

    steps = [(at, k) for at in range(count) for k in range(5)]
    load(0).wait()
    move(*weights[0], 14).wait()
    arrange(0)
    for t in range(len(steps) + 2):
        work = []
        if t + 1 < len(PIECES):
            load(t + 1).wait()
        if t == 1:
            for k in range(1, 4):
                move(*weights[k], 14 + k).wait()
        if t >= 2:
            at, k = steps[t - 2]
            if THIRDS[k]:
                third(at, THIRDS[k])
                work += [(at, 2, THIRDS[k], 448), (at, 3, THIRDS[k], 448)]
        if 1 <= t <= len(steps):
            at, k = steps[t - 1]
            second(at, SECONDS[k])
            work.append((at, 1, SECONDS[k], 576))
        if t < len(steps):
            at, k = steps[t]
            if t + 1 < len(PIECES):
                arrange(t + 1)
            first(at, QUADS[k])
            work.append((at, 0, QUADS[k], A1_QROW))
        for item in work:
            send(*item)
        if t == 4 and arrange_here:
            move(xs, xs_out, 8).start()
    for at in range(count):
        for which in range(4):
            move(kept[at][which], outs[at][which], 4 * at + which).wait()
    if arrange_here:
        move(xs, xs_out, 8).wait()


def forward(chunk, nets, pixels, perm, w1, w2, w3a, w3b, deps=()):
    arrange_here = pixels.ndim == 3
    ins = [w1, w2, w3a, w3b, *deps]
    outs = [jax.ShapeDtypeStruct((PIX * PIX if arrange_here else 16, LANES), BF)]
    outs += [jax.ShapeDtypeStruct((r, LANES), BF) for r in KEPT] * len(nets)
    res = pl.pallas_call(
        functools.partial(forward_kernel, chunk, nets, arrange_here),
        grid=(1,),
        in_specs=[pl.BlockSpec(memory_space=pl.ANY), whole(perm)] + waits(ins),
        out_specs=waits(outs),
        out_shape=outs,
        scratch_shapes=[pltpu.VMEM((r, LANES), BF) for r in KEPT * len(nets)]
        + [pltpu.VMEM((r, LANES), BF) for r in (A1_ROWS, A2_ROWS) * len(nets)]
        + [pltpu.VMEM((PIX * PIX, LANES), BF)]
        + [pltpu.VMEM((GROUP, PIX * PIX if arrange_here else 16, STEPS), BF)]
        + [pltpu.VMEM(w.shape, BF) for w in (w1, w2, w3a, w3b)]
        + [pltpu.SemaphoreType.DMA((18,))],
        compiler_params=pltpu.CompilerParams(vmem_limit_bytes=VMEM_LIMIT),
        cost_estimate=cost(12 * len(nets)),
        name="forward",
    )(pixels, perm, *ins)
    return res[0], [res[1 + 4 * k : 5 + 4 * k] for k in range(len(nets))]


def lanes_of(c):
    return pl.ds(c * LANES, LANES)


def embed_kernel(chunks, slabs, ids, *refs):
    feats, dense = refs[:chunks], refs[chunks : chunks + slabs]
    embed, embeddings, f, d, sems = refs[-5:]

    def feat(c, k):
        return pltpu.make_async_copy(
            feats[c].at[ids[k]], f.at[k, :, lanes_of(c)], sems.at[c, k]
        )

    def matrix(k):
        return pltpu.make_async_copy(dense[k], d.at[k], sems.at[chunks, k])

    for k in range(slabs):
        for c in range(chunks):
            feat(c, k).start()
        matrix(k).start()
    total = None
    for k in range(slabs):
        for c in range(chunks):
            feat(c, k).wait()
        matrix(k).wait()
        part = dot_tn(d[k], f[k])
        total = part if total is None else total + part
    embed[...] = total
    embeddings[...] = total.astype(BF).T


def embed_call(ids, feats, dense, deps=()):
    chunks, slabs = len(feats), len(dense)
    count = chunks * LANES
    outs = [jax.ShapeDtypeStruct((HID, count), F32), jax.ShapeDtypeStruct((count, HID), BF)]
    ins = [*feats, *dense, *deps]
    return pl.pallas_call(
        functools.partial(embed_kernel, chunks, slabs),
        grid_spec=pltpu.PrefetchScalarGridSpec(
            num_scalar_prefetch=1,
            grid=(1,),
            in_specs=waits(ins),
            out_specs=[whole(o) for o in outs],
            scratch_shapes=[
                pltpu.VMEM((slabs, feats[0].shape[1], count), BF),
                pltpu.VMEM((slabs, *dense[0].shape), BF),
                pltpu.SemaphoreType.DMA((chunks + 1, slabs)),
            ],
        ),
        out_shape=outs,
        compiler_params=pltpu.CompilerParams(vmem_limit_bytes=VMEM_LIMIT),
        cost_estimate=cost(5),
        name="embed",
    )(ids, *ins)


def discounted(rewards, done):
    carry = (GAMMA * TRACE) * (1.0 - done.astype(F32))
    step = lax.broadcasted_iota(jnp.int32, rewards.shape, 1) % STEPS
    carry = jnp.where(step == STEPS - 1, 0.0, carry)
    shift, count = 1, rewards.shape[1]
    while shift < STEPS:
        rewards = rewards + carry * pltpu.roll(rewards, count - shift, 1)
        carry = carry * pltpu.roll(carry, count - shift, 1)
        shift *= 2
    return rewards


def heads_kernel(chunks, slabs, depth, ids, *refs):
    feats, refs = refs[:chunks], refs[chunks:]
    dense_t, refs = refs[:slabs], refs[slabs:]
    dense1, refs = refs[:slabs], refs[slabs:]
    embed, done, rewards, returns, refs = *refs[:4], refs[4:]
    gfeats, refs = refs[:chunks], refs[chunks:]
    grads, refs = refs[:slabs], refs[slabs:]
    deeper, f, one, target, emb, gout, gone, gdeep, mid, sems, outs = refs
    share = HID // slabs
    wide = gone.shape[2]
    spots = [pl.ds(pl.multiple_of(ids[k] * share, 64), share) for k in range(slabs)]

    def move(source, into, at):
        return pltpu.make_async_copy(source, into, sems.at[at])

    def feat(c, k):
        return move(feats[c].at[ids[k]], f.at[k, :, lanes_of(c)], c * slabs + k)

    def matrix(k):
        return move(dense1[k], one.at[k], chunks * slabs + k)

    def other(k):
        return move(dense_t[k], target.at[k], (chunks + 1) * slabs + k)

    def result(c, net, k):
        return pltpu.make_async_copy(
            gout.at[net, k, :, lanes_of(c)], gfeats[c].at[net, ids[k]],
            outs.at[c * slabs + k, net],
        )

    def gradient(k):
        return pltpu.make_async_copy(gone.at[k], grads[k], outs.at[chunks * slabs + k, 0])

    late = pltpu.make_async_copy(gdeep, deeper, outs.at[chunks * slabs, 1])
    given = move(embed, emb, (chunks + 2) * slabs)

    for k in range(slabs):
        for c in range(chunks):
            feat(c, k).start()
        matrix(k).start()
    given.start()
    for k in range(slabs):
        other(k).start()

    hidden = None
    for k in range(slabs):
        for c in range(chunks):
            feat(c, k).wait()
        matrix(k).wait()
        part = dot_nn(one[k, :, :depth], f[k])
        hidden = part if hidden is None else hidden + part
    h1, slope1 = silu_pair(hidden)
    h1 = h1.astype(BF)
    for k in range(slabs):
        mid[spots[k], :] = dot_tn(one[k, :, wide : wide + share], h1)
    h2, slope2 = silu_pair(mid[...])
    h2 = h2.astype(BF)
    for k in range(slabs):
        mid[spots[k], :] = dot_tn(one[k, :, wide + share :], h2)
    given.wait()
    differ = mid[...] - emb[...]
    reward = jnp.sum(differ * differ, axis=0, keepdims=True) * (1.0 / HID)
    rewards[...] = reward
    returns[...] = discounted(reward, done[...])
    mid[...] = differ
    g_pred = differ.astype(BF)
    minus = (-differ).astype(BF)
    grad = None
    for k in range(slabs):
        part = dot_nn(one[k, :, wide + share :], mid[spots[k], :].astype(BF))
        grad = part if grad is None else grad + part
    grad = grad * slope2
    g_second = grad.astype(BF)
    mid[...] = grad
    grad = None
    for k in range(slabs):
        part = dot_nn(one[k, :, wide : wide + share], mid[spots[k], :].astype(BF))
        grad = part if grad is None else grad + part
    g_hidden = (grad * slope1).astype(BF)

    for k in range(slabs):
        if wide > depth:
            gone[k, :, depth:] = jnp.zeros((HID, wide - depth), BF)
        gone[k, :, :depth] = dot_nt(g_hidden, f[k]).astype(BF)
        gradient(k).start()
    gdeep[:, :HID] = dot_nt(h1, g_second).astype(BF)
    gdeep[:, HID:] = dot_nt(h2, g_pred).astype(BF)
    late.start()
    for k in range(slabs):
        gout[1, k] = dot_tn(one[k, :, :depth], g_hidden).astype(BF)
        for c in range(chunks):
            result(c, 1, k).start()
    for k in range(slabs):
        other(k).wait()
        gout[0, k] = dot_nn(target[k], minus).astype(BF)
        for c in range(chunks):
            result(c, 0, k).start()
    late.wait()
    for k in range(slabs):
        gradient(k).wait()
        for c in range(chunks):
            for net in range(2):
                result(c, net, k).wait()


def heads(ids, feats, dense_t, dense1, embed, done):
    chunks, slabs = len(feats), len(dense1)
    count = chunks * LANES
    depth = feats[0].shape[1]
    wide = dense1[0].shape[1] - 2 * (HID // slabs)
    line = jax.ShapeDtypeStruct((1, count), F32)
    outs = [
        line,
        line,
        *[jax.ShapeDtypeStruct((2, *f.shape), BF) for f in feats],
        *[jax.ShapeDtypeStruct((HID, wide), BF)] * slabs,
        jax.ShapeDtypeStruct((HID, 2 * HID), BF),
    ]
    ins = [*feats, *dense_t, *dense1, embed]
    res = pl.pallas_call(
        functools.partial(heads_kernel, chunks, slabs, depth),
        grid_spec=pltpu.PrefetchScalarGridSpec(
            num_scalar_prefetch=1,
            grid=(1,),
            in_specs=waits(ins) + [whole(done)],
            out_specs=[whole(line)] * 2 + waits(outs[2:]),
            scratch_shapes=[
                pltpu.VMEM((slabs, depth, count), BF),
                pltpu.VMEM((slabs, *dense1[0].shape), BF),
                pltpu.VMEM((slabs, *dense_t[0].shape), BF),
                pltpu.VMEM((HID, count), F32),
                pltpu.VMEM((2, slabs, depth, count), BF),
                pltpu.VMEM((slabs, HID, wide), BF),
                pltpu.VMEM((HID, 2 * HID), BF),
                pltpu.VMEM((HID, count), F32),
                pltpu.SemaphoreType.DMA(((chunks + 2) * slabs + 1,)),
                pltpu.SemaphoreType.DMA(((chunks + 1) * slabs, 2)),
            ],
        ),
        out_shape=outs,
        compiler_params=pltpu.CompilerParams(vmem_limit_bytes=VMEM_LIMIT),
        cost_estimate=cost(15),
        name="heads",
    )(ids, *ins, done)
    return res[0], res[1], res[2 : 2 + chunks], res[2 + chunks : -1], res[-1]


def edges_zero(ref, side, channels, top, bottom):
    line = side * channels
    spots = [(0, top * line), ((side - bottom) * line, bottom * line)]
    for i in range(top, side - bottom):
        spots += [(i * line, top * channels), ((i + 1) * line - bottom * channels, bottom * channels)]
    for start, size in spots:
        if size:
            ref[start : start + size, :] = jnp.zeros((size, LANES), BF)


def deep_product(i, g, s3, d3p):
    part = slice(i * 448, i * 448 + 448)
    d3p[((i + 2) * 11 + 2) * 64 : ((i + 2) * 11 + 9) * 64, :] = (
        g[part, :].astype(F32) * s3[part, :].astype(F32)
    ).astype(BF)


def deep_row(i, s2, v3, d3p, d2p, a2=None):
    for b in range(3):
        window = stack([rows(d3p, ((i + r) * 11 + 3 * b) * 64, 320) for r in range(3)])
        up = dot_nn(v3[...], window)
        slope = rows(s2, (i * 9 + 3 * b) * 64, 192).astype(F32)
        if a2 is not None:
            act, slope = silu_half(slope)
            put(a2, (i * 10 + 3 * b) * 64, 192, act.astype(BF))
        put(d2p, ((i + 1) * 11 + 3 * b + 1) * 64, 192, (up * slope).astype(BF))


D1_LINE = 22 * C1
D1_ROWS = 22 * D1_LINE


def first_rows(m, s1, v2, d2p, d1, a1=None):
    for n in range(10):
        window = stack([rows(d2p, ((m + a) * 11 + n) * 64, 128) for a in range(2)])
        slope = rows(s1, (m * 10 + n) * 128, 128, 128).astype(F32)
        if a1 is not None:
            act, slope = silu_half(slope)
            put(a1, (m * 10 + n) * 128, 128, act.astype(BF))
        grad = (dot_nn(v2[...], window) * slope).astype(BF)
        for dr in range(2):
            at = (2 * m + 1 + dr) * D1_LINE + (2 * n + 1) * C1
            put(d1, at, 64, grad[dr * 64 : dr * 64 + 64, :], 32)


def learner_kernel(add, g_in, s3_in, h2_in, h1_in, xs_in, v3, v2, s1hot, *refs):
    before = refs[0] if add else None
    d1_out, grads = refs[-16:-14]
    g, s3, h2, h1, a2, a1, xs, d1, d3p, d2p, sum1, sum2, sum3, sems = refs[-14:]

    def move(source, target, index):
        return pltpu.make_async_copy(source, target, sems.at[index])

    def pair(v):
        return pl.ds(v * 2 * A1_QROW, 2 * A1_QROW)

    def line(m):
        return pl.ds((2 * m + 1) * D1_LINE, 2 * D1_LINE)

    tops = [pl.ds(0, 4 * 448), pl.ds(4 * 448, 3 * 448)]

    middles = [pl.ds(0, 4 * 576), pl.ds(4 * 576, 5 * 576)]

    for k, part in enumerate(tops):
        move(g_in.at[1, part], g.at[part], 2 * k).start()
        move(s3_in.at[part], s3.at[part], 2 * k + 1).start()
        move(h2_in.at[middles[k]], h2.at[middles[k]], 4 + k).start()
        move(h1_in.at[pair(k)], h1.at[pair(k)], 6 + k).start()
    move(xs_in, xs, 12).start()
    for v in range(2, 5):
        move(h1_in.at[pair(v)], h1.at[pair(v)], 6 + v).start()
    edges_zero(d3p, 11, C3, 2, 2)
    edges_zero(d2p, 11, C2, 1, 1)
    edges_zero(d1, 22, C1, 1, 1)
    edges_zero(a2, 10, C2, 0, 1)
    sum1[...] = jnp.zeros_like(sum1)
    sum2[...] = jnp.zeros_like(sum2)
    sum3[...] = jnp.zeros_like(sum3)

    def wait_top(k):
        part = tops[k]
        move(g_in.at[1, part], g.at[part], 2 * k).wait()
        move(s3_in.at[part], s3.at[part], 2 * k + 1).wait()

    def conv3_terms(u):
        left = jnp.concatenate(
            [
                stack([rows(d3p, ((2 * u + 2 + r) * 11 + 2 * b + 2) * 64, 128) for r in range(2)])
                for b in range(4)
            ],
            axis=1,
        )
        right = jnp.concatenate(
            [
                stack([rows(a2, ((2 * u + r) * 10 + 2 * b) * 64, 256) for r in range(4)])
                for b in range(4)
            ],
            axis=1,
        )
        sum3[...] += dot_nt(left, right)

    def conv2_terms(m):
        left = jnp.concatenate(
            [
                stack([rows(d2p, ((m + r) * 11 + 2 * b) * 64, 192) for r in range(2)])
                for b in range(5)
            ],
            axis=1,
        )
        right = jnp.concatenate([rows(a1, m * A1_QROW + b * 256, 256) for b in range(5)], axis=1)
        sum2[...] += dot_nt(left, right)

    def conv1_terms(m):
        left = jnp.concatenate(
            [
                stack(
                    [
                        rows(d1, (2 * m + 1 + dr) * D1_LINE + (4 * b + 1) * C1, 128)
                        for dr in range(2)
                    ]
                )
                for b in range(5)
            ],
            axis=1,
        )
        right = jnp.concatenate(
            [
                stack([rows(xs, ((2 * m + r) * 21 + 4 * b) * 16, 80) for r in range(3)])
                for b in range(5)
            ],
            axis=1,
        )
        sum1[...] += dot_nt(left, right)

    def wait_pairs(*pairs):
        for v in pairs:
            move(h1_in.at[pair(v)], h1.at[pair(v)], 6 + v).wait()

    def send(*lines):
        for m in lines:
            move(d1.at[line(m)], d1_out.at[line(m)], 11).start()

    wait_top(0)
    for i in range(12):
        if i == 1:
            move(h2_in.at[middles[0]], h2.at[middles[0]], 4).wait()
        if i == 2:
            wait_pairs(0)
        if i == 4:
            wait_top(1)
            move(h2_in.at[middles[1]], h2.at[middles[1]], 5).wait()
            wait_pairs(1)
            move(xs_in, xs, 12).wait()
        if i == 6:
            wait_pairs(2)
            send(0, 1)
        if i == 8:
            wait_pairs(3, 4)
            send(2, 3)
        if i == 10:
            send(4, 5)
        if i < 7:
            deep_product(i, g, s3, d3p)
        if 1 <= i <= 9:
            deep_row(i - 1, h2, v3, d3p, d2p, a2)
        if i >= 3:
            conv2_terms(i - 3)
        if 2 <= i:
            first_rows(i - 2, h1, v2, d2p, d1, a1)
        if i >= 4:
            conv1_terms(i - 4)
        if i in (5, 7, 9, 10):
            conv3_terms((5, 7, 9, 10).index(i))
    send(6, 7, 8, 9)
    for edge in (slice(0, D1_LINE), slice(21 * D1_LINE, D1_ROWS)):
        move(d1.at[edge], d1_out.at[edge], 11).start()
    conv2_terms(9)
    conv1_terms(8)
    conv1_terms(9)

    grads[...] = jnp.zeros_like(grads) if before is None else before[...]
    total = jnp.zeros((64, 32), F32)
    for pos in range(8):
        block = sum1[pos * 32 : pos * 32 + 32, :]
        high = block.astype(BF)
        rest = block - high.astype(F32)
        mid = rest.astype(BF)
        low = (rest - mid.astype(F32)).astype(BF)
        r, c = divmod(pos, 4)
        hot = s1hot[(c // 2) * 4 + r * 2 + c % 2]
        total = total + (dot_nt(hot, high) + (dot_nt(hot, mid) + dot_nt(hot, low)))
    grads[576:640, 0:32] += total
    for rp in range(2):
        for qq in range(2):
            block = None
            for q in range(2):
                dj = q + 1 - qq
                at = ((1 - rp) * 3 + dj) * 64
                part = sum2[at : at + 64, q * 128 : q * 128 + 128]
                block = part if block is None else block + part
            block = block.T
            for d in range(4):
                tap = (2 * rp + d // 2) * 4 + 2 * qq + d % 2
                grads[tap * 32 : tap * 32 + 32, 64:128] += block[d * 32 : d * 32 + 32, :]
    for kr in range(3):
        block = None
        for pr in range(2):
            for pc in range(2):
                at = (pr * 2 + pc) * 64
                lane = (pr + kr) * 256 + pc * 64
                part = sum3[at : at + 64, lane : lane + 192]
                block = part if block is None else block + part
        grads[kr * 192 : kr * 192 + 192, 0:64] += block.T
    move(d1, d1_out, 11).wait()


PACKED = 768


def learner_backward(gfeat, s3, h2, h1, xs, v3, v2, before, deps=()):
    fixed = lambda s: pl.BlockSpec(s, lambda i: (0,) * len(s))
    learner = lambda a: pl.BlockSpec((None, *a.shape[1:]), lambda i: (1, 0, 0))
    s1hot = jnp.asarray(first_taps(), BF)
    before = [] if before is None else [before]
    return pl.pallas_call(
        functools.partial(learner_kernel, bool(before)),
        grid=(1,),
        in_specs=[pl.BlockSpec(memory_space=pl.ANY)] * 5
        + [learner(v3), learner(v2), fixed(s1hot.shape)]
        + [fixed((PACKED, 128))] * len(before)
        + waits(deps),
        out_specs=[pl.BlockSpec(memory_space=pl.ANY), fixed((PACKED, 128))],
        out_shape=[
            jax.ShapeDtypeStruct((D1_ROWS, LANES), BF),
            jax.ShapeDtypeStruct((PACKED, 128), F32),
        ],
        scratch_shapes=[
            pltpu.VMEM((r, LANES), BF)
            for r in (
                FEAT, FEAT, A2_ROWS, A1_ROWS, A2P_ROWS, A1_ROWS, PIX * PIX, D1_ROWS,
                PAD_ROWS, PAD_ROWS,
            )
        ]
        + [
            pltpu.VMEM((256, 240), F32),
            pltpu.VMEM((384, 256), F32),
            pltpu.VMEM((256, 1024), F32),
            pltpu.SemaphoreType.DMA((13,)),
        ],
        compiler_params=pltpu.CompilerParams(vmem_limit_bytes=VMEM_LIMIT),
        cost_estimate=cost(20),
        name="learner_backward",
    )(gfeat, s3, h2, h1, xs, v3, v2, s1hot, *before, *deps)


def pixel_kernel(chunk, g_in, s3_in, s2_in, s1_in, d1_in, v3, v2, v1, perm, *refs):
    out_all = refs[-12]
    g, s3, s2, s1, mine, theirs, d3p, d2p, dxs, out, sems = refs[-11:]

    def move(source, target, index):
        return pltpu.make_async_copy(source, target, sems.at[index])

    def pair(v):
        return pl.ds(v * 2 * A1_QROW, 2 * A1_QROW)

    def line(v):
        return pl.ds((4 * v + 1) * D1_LINE, 4 * D1_LINE)

    def band(v):
        return pl.ds(v * 4 * PATCH_ROWS, (4 if v < 4 else 5) * PATCH_ROWS)

    here = pl.ds(chunk * GROUP, GROUP)
    tops = [pl.ds(0, 4 * 448), pl.ds(4 * 448, 3 * 448)]

    middles = [pl.ds(0, 4 * 576), pl.ds(4 * 576, 5 * 576)]

    for k, part in enumerate(tops):
        move(g_in.at[0, part], g.at[part], 2 * k).start()
        move(s3_in.at[part], s3.at[part], 2 * k + 1).start()
        move(s2_in.at[middles[k]], s2.at[middles[k]], 14 + k).start()
        move(s1_in.at[pair(k)], s1.at[pair(k)], 4 + k).start()
        move(d1_in.at[line(k)], theirs.at[line(k)], 9 + k).start()
    edges_zero(d3p, 11, C3, 2, 2)
    edges_zero(d2p, 11, C2, 1, 1)
    edges_zero(mine, 22, C1, 1, 1)
    theirs[:D1_LINE, :] = jnp.zeros((D1_LINE, LANES), BF)

    def wait_top(k):
        part = tops[k]
        move(g_in.at[0, part], g.at[part], 2 * k).wait()
        move(s3_in.at[part], s3.at[part], 2 * k + 1).wait()

    def patches(v):
        for b in range(7):
            window = stack(
                [
                    rows(ref, (4 * v + r) * D1_LINE + 3 * b * C1, 128, 32)
                    for ref in (mine, theirs)
                    for r in range(5)
                ]
            )
            dx = dot_nn(v1[...], window).astype(BF)
            for pr in range(4):
                put(dxs, ((4 * v + pr) * 21 + 3 * b) * 16, 48, dx[pr * 48 : pr * 48 + 48], 16)

    def last_patches():
        w = jnp.concatenate([v1[:48, 0:128], v1[:48, 640:768]], axis=1)
        for b in range(7):
            at = slice(20 * D1_LINE + 3 * b * C1, 20 * D1_LINE + 3 * b * C1 + 128)
            window = stack([mine[at, :], theirs[at, :]])
            put(dxs, (20 * 21 + 3 * b) * 16, 48, dot_nn(w, window).astype(BF), 16)

    def turn(p):
        part = slice(p * PATCH_ROWS, (p + 1) * PATCH_ROWS)
        block = dot_tn(perm[...], dxs[part, :]).astype(BF)
        for e in range(GROUP):
            out[e, part, :] = block[:, e * STEPS : (e + 1) * STEPS]

    def wait_pairs(*pairs):
        for v in pairs:
            move(s1_in.at[pair(v)], s1.at[pair(v)], 4 + v).wait()
            move(d1_in.at[line(v)], theirs.at[line(v)], 9 + v).wait()

    for v in range(2, 5):
        move(s1_in.at[pair(v)], s1.at[pair(v)], 4 + v).start()
        move(d1_in.at[line(v)], theirs.at[line(v)], 9 + v).start()
    wait_top(0)
    for i in range(15):
        if i == 1:
            move(s2_in.at[middles[0]], s2.at[middles[0]], 14).wait()
        if i == 2:
            wait_pairs(0)
        if i == 4:
            wait_top(1)
            move(s2_in.at[middles[1]], s2.at[middles[1]], 15).wait()
            wait_pairs(1, 2)
        if i == 8:
            wait_pairs(3, 4)
        if i == 11:
            for v in (0, 1):
                move(out.at[:, band(v)], out_all.at[here, band(v)], 16).start()
        if i == 13:
            for v in (2, 3):
                move(out.at[:, band(v)], out_all.at[here, band(v)], 16).start()
        if i < 7:
            deep_product(i, g, s3, d3p)
        if i >= 6 and i % 2 == 0:
            v = (i - 6) // 2
            for p in range(4 * v, 4 * v + (4 if v < 4 else 5)):
                turn(p)
        if 1 <= i <= 9:
            deep_row(i - 1, s2, v3, d3p, d2p)
        if 4 <= i <= 12 and i % 2 == 0:
            v = (i - 4) // 2
            patches(v)
            if v == 4:
                last_patches()
        if 2 <= i <= 11:
            first_rows(i - 2, s1, v2, d2p, mine)
    move(out.at[:, band(4)], out_all.at[here, band(4)], 16).start()
    move(out, out_all.at[here], 16).wait()


def pixel_backward(chunk, envs, gfeat, s3, s2, s1, d1, v3, v2, v1, perm, before, deps=()):
    fixed = lambda s: pl.BlockSpec(s, lambda i: (0,) * len(s))
    target = lambda a: pl.BlockSpec((None, *a.shape[1:]), lambda i: (0, 0, 0))
    ins = [gfeat, s3, s2, s1, d1, v3, v2, v1, perm]
    specs = [pl.BlockSpec(memory_space=pl.ANY)] * 5
    specs += [target(v3), target(v2), fixed(v1.shape), fixed(perm.shape)]
    aliases = {}
    if before is not None:
        aliases = {len(ins): 0}
        ins.append(before)
        specs.append(pl.BlockSpec(memory_space=pl.ANY))
    ins += deps
    specs += waits(deps)
    return pl.pallas_call(
        functools.partial(pixel_kernel, chunk),
        grid=(1,),
        in_specs=specs,
        out_specs=pl.BlockSpec(memory_space=pl.ANY),
        out_shape=jax.ShapeDtypeStruct((envs, PIX * PIX, STEPS), BF),
        scratch_shapes=[
            pltpu.VMEM((r, LANES), BF)
            for r in (
                FEAT, FEAT, A2_ROWS, A1_ROWS, D1_ROWS, D1_ROWS, PAD_ROWS, PAD_ROWS, PIX * PIX,
            )
        ]
        + [pltpu.VMEM((GROUP, PIX * PIX, STEPS), BF), pltpu.SemaphoreType.DMA((17,))],
        input_output_aliases=aliases,
        compiler_params=pltpu.CompilerParams(vmem_limit_bytes=VMEM_LIMIT),
        cost_estimate=cost(20),
        name="pixel_backward",
    )(*ins)


def pack(index, dense1, dense2, dense3, wide, copies, parts, cores):
    lines, depth = dense1.shape
    share = HID // parts
    chips = parts // cores

    def kernel(at, one, two, three, out, ids):
        for k in range(cores):
            for j in range(chips):
                chip = lax.rem(at[0] // cores + chips - j, chips)
                ids[k * chips + j] = chip * cores + lax.rem(at[0] + k, cores)
        out[0] = jnp.zeros_like(out[0])
        out[0, :, :depth] = one[...]
        for q in range(parts):

            @pl.when(at[0] == q)
            def _():
                out[0, :, wide : wide + share] = two[:, q * share : (q + 1) * share]
                out[0, :, wide + share :] = three[:, q * share : (q + 1) * share]

        for k in range(1, copies):
            out[k] = out[0]

    result = jax.ShapeDtypeStruct((copies, lines, wide + 2 * share), BF)
    return pl.pallas_call(
        kernel,
        grid_spec=pltpu.PrefetchScalarGridSpec(
            num_scalar_prefetch=1,
            grid=(1,),
            in_specs=[whole(dense1), whole(dense2), whole(dense3)],
            out_specs=[whole(result), pl.BlockSpec(memory_space=pltpu.SMEM)],
        ),
        out_shape=[result, jax.ShapeDtypeStruct((parts,), jnp.int32)],
        cost_estimate=cost(1),
        name="pack",
    )(index, dense1, dense2, dense3)


def join(left, right, deps):
    count = len(left)

    def kernel(*refs):
        for k in range(count):
            total = refs[k][...].astype(F32) + refs[count + k][...].astype(F32)
            refs[-count + k][...] = total.astype(BF)

    lines, wide = left[0].shape
    block = pl.BlockSpec((lines // 2, wide), lambda i: (i, 0))
    return pl.pallas_call(
        kernel,
        grid=(2,),
        in_specs=[block] * (2 * count) + waits(deps),
        out_specs=[block] * count,
        out_shape=[jax.ShapeDtypeStruct((lines, wide), BF)] * count,
        cost_estimate=cost(2),
        name="join",
    )(*left, *right, *deps)


def split(arrays, index, groups, parts, deps, terms=()):
    lines, wide = arrays[0].size // (arrays[0].shape[-1] * groups * parts), arrays[0].shape[-1]
    arrays = [a.reshape(groups, parts, lines, wide) for a in arrays]
    count = len(arrays)
    outs = [jax.ShapeDtypeStruct((groups, lines, wide), BF)] * parts
    outs += [jax.ShapeDtypeStruct(t.shape[1:], BF) for t in terms]
    results = len(outs)

    def kernel(at, *refs):
        for j in range(parts):
            source = lax.rem(at[0] + j, parts)
            for i in range(groups):
                total = refs[0][i, source].astype(F32)
                for k in range(1, count):
                    total = total + refs[k][i, source].astype(F32)
                refs[len(refs) - results + j][i] = total.astype(BF)
        for k in range(len(terms)):
            total = jnp.sum(refs[count + k][...].astype(F32), axis=0)
            refs[len(refs) - len(terms) + k][...] = total.astype(BF)

    return pl.pallas_call(
        kernel,
        grid_spec=pltpu.PrefetchScalarGridSpec(
            num_scalar_prefetch=1,
            grid=(1,),
            in_specs=[whole(a) for a in (*arrays, *terms)] + waits(deps),
            out_specs=[whole(o) for o in outs],
        ),
        out_shape=outs,
        cost_estimate=cost(2),
        name="split",
    )(index, *arrays, *terms, *deps)


def middle(blocks, depth, scale, small, deps):
    count = len(blocks)

    def kernel(*refs):
        total = refs[0][...].astype(F32)
        for k in range(1, count):
            total = total + refs[k][...].astype(F32)
        refs[-2][...] = total[:, :depth] * scale
        share = jnp.sum(refs[count][...], axis=0) * (0.5 * scale)
        refs[-1][...] = jnp.broadcast_to(share[None], refs[-1].shape)

    ins = [*blocks, small]
    outs = [
        jax.ShapeDtypeStruct((blocks[0].shape[0], depth), F32),
        jax.ShapeDtypeStruct(small.shape, small.dtype),
    ]
    return pl.pallas_call(
        kernel,
        grid=(1,),
        in_specs=[whole(a) for a in ins] + waits(deps),
        out_specs=[whole(a) for a in outs],
        out_shape=outs,
        cost_estimate=cost(2),
        name="middle",
    )(*ins, *deps)


def finish(deeper, scale, small, deps):
    count = len(deeper)

    def kernel(*refs):
        terms = [refs[k][...].astype(F32) for k in range(count)]
        while len(terms) > 1:
            joined = [a + b for a, b in zip(terms[::2], terms[1::2])]
            terms = joined + terms[len(joined) * 2 :]
        total = terms[0] * scale
        packed = refs[count]
        two, three, one, conv2, conv3 = refs[-5:]
        two[...] = total[:, :HID]
        three[...] = total[:, HID:]
        one[...] = packed[576:640, :C1]
        conv2[...] = packed[:512, 64:]
        conv3[...] = packed[:576, :64]

    ins = [*deeper, small]
    lines = deeper[0].shape[0]
    outs = [
        jax.ShapeDtypeStruct(s, F32)
        for s in ((lines, HID), (lines, HID), (64, C1), (512, C2), (576, C3))
    ]
    return pl.pallas_call(
        kernel,
        grid=(1,),
        in_specs=[whole(a) for a in ins] + waits(deps),
        out_specs=[whole(a) for a in outs],
        out_shape=outs,
        cost_estimate=cost(2),
        name="finish",
    )(*ins, *deps)


def shards(
    frames,
    episode_done,
    target_conv1,
    target_conv2,
    target_conv3,
    target_dense,
    predictor_conv1,
    predictor_conv2,
    predictor_conv3,
    predictor_dense1,
    predictor_dense2,
    predictor_dense3,
):
    everyone = ("dp", "mp")
    dp, mp = lax.axis_size("dp"), lax.axis_size("mp")
    envs_here = frames.shape[0]
    count = envs_here * STEPS
    chunks = count // LANES
    grad_scale = 1.0 / math.sqrt(count * dp * mp)
    cores = 2 if mp % 2 == 0 else 1
    chips = mp // cores
    pairs = 2 if dp % 2 == 0 else 1
    depth = target_dense.shape[0]
    wide = -(-depth // 128) * 128

    def from_chip(value, j):
        moves = [(i, ((i // cores + j) % chips) * cores + i % cores) for i in range(mp)]
        return lax.ppermute(value, "mp", moves)

    def other_core(value):
        return lax.ppermute(value, "mp", [(i, i ^ 1) for i in range(mp)])

    here = lax.axis_index("mp")
    place = lax.axis_index("dp")

    x = frames.swapaxes(1, 2)
    perm = jnp.asarray(patch_order(), BF)
    mine, ids = pack(
        here.reshape(1), predictor_dense1.T, predictor_dense2, predictor_dense3, wide, dp, mp, cores
    )
    mine = lax.all_to_all(mine, "dp", split_axis=0, concat_axis=0, tiled=True)
    mine = mine.reshape(HID, mine.shape[2])
    dense_t = [target_dense] + [from_chip(target_dense, j) for j in range(1, chips)]
    w1, w2, w3a, w3b, v3, v2, v1 = make_weights(
        (target_conv1, target_conv2, target_conv3),
        (predictor_conv1, predictor_conv2, predictor_conv3),
    )
    fixed = (perm, w1, w2, w3a, w3b)
    xs, (learner, target) = forward(0, (1, 0), x, *fixed)
    saved = [(xs, learner, target)]
    mine = after(mine, target[2], *dense_t[1:])
    dense_t += [other_core(d) for d in dense_t] if cores == 2 else []
    dense1 = [mine] + [from_chip(mine, j) for j in range(1, chips)]
    for c in range(1, chunks):
        xs, (learner, target) = forward(c, (1, 0), x, *fixed, [mine])
        saved.append((xs, learner, target))
    feats = [[sv[k][2].reshape(mp, depth, LANES) for sv in saved] for k in (2, 1)]
    embed, embeddings = embed_call(ids, feats[0], dense_t)
    dense1[1:] = [after(d, embed) for d in dense1[1:]]
    dense1 += [other_core(d) for d in dense1] if cores == 2 else []
    rewards, returns, gfeats, grads, deeper = heads(
        ids, feats[1], dense_t, dense1, embed, episode_done.reshape(1, count)
    )
    gfeats = [g.reshape(2, FEAT, LANES) for g in gfeats]

    deeper = deeper.reshape(dp, HID // dp, 2 * HID)
    deeper = lax.all_to_all(deeper, "dp", split_axis=0, concat_axis=0, tiled=True)
    kept = grads[:chips]
    terms = [kept[0]]
    if cores == 2:
        got = [other_core(g) for g in grads[chips:][::-1]][::-1]
        terms.append(got[0])
        kept = [kept[0]] + (list(join(kept[1:], got[1:], [])) if chips > 1 else [])
    terms += [from_chip(kept[j], chips - j) for j in range(1, chips)]
    def learner_part(c, small, deps):
        xs, (h1, h2, _, s3), _ = saved[c]
        return learner_backward(gfeats[c], s3, h2, h1, xs, v3, v2, small, deps)

    def pixel_part(c, frame_grad, deps):
        s1, s2, _, s3 = saved[c][2]
        return pixel_backward(
            c, envs_here, gfeats[c], s3, s2, s1, first[c], v3, v2, v1, perm, frame_grad, deps
        )

    first, small = learner_part(0, None, kept[1:])
    first = [first]
    groups = dp // pairs
    total = split(terms, (place % pairs).reshape(1), groups, pairs, [small])
    got = [
        lax.ppermute(total[j], "dp", [(i, i - i % pairs + (i + j) % pairs) for i in range(dp)])
        for j in range(1, pairs)
    ]
    for c in range(1, chunks):
        grad, small = learner_part(c, small, total)
        first.append(grad)
    small = small.reshape(dp * mp, PACKED // (dp * mp), 128)
    spread = lax.all_to_all(small, everyone, split_axis=0, concat_axis=0, tiled=True)
    *total, deeper = split(
        [total[0], *got], (place // pairs).reshape(1), 1, groups, [small], [deeper]
    )
    total = [t.reshape(t.shape[1:]) for t in total]
    got = [
        lax.ppermute(total[j], "dp", [(i, (i + j * pairs) % dp) for i in range(dp)])
        for j in range(1, groups)
    ]

    partner = (lambda i, j: i ^ j) if mp & (mp - 1) == 0 else (lambda i, j: (i + j) % mp)
    deeper = [deeper] + [
        lax.ppermute(deeper, "mp", [(i, partner(i, j)) for i in range(mp)]) for j in range(1, mp)
    ]

    frame_grad = pixel_part(0, None, total)
    d1, share = middle([total[0], *got], depth, grad_scale, spread, [frame_grad])
    small = lax.all_to_all(share, everyone, split_axis=0, concat_axis=0, tiled=True)
    for c in range(1, chunks):
        frame_grad = pixel_part(c, frame_grad, [share])
    d2, d3, e1, e2, e3 = finish(deeper, grad_scale, small.reshape(PACKED, 128), [frame_grad])
    return (
        embeddings.reshape(envs_here, STEPS, HID),
        rewards.reshape(envs_here, STEPS),
        returns.reshape(envs_here, STEPS),
        e1.reshape(8, 8, 1, C1),
        e2.reshape(4, 4, C1, C2),
        e3.reshape(3, 3, C2, C3),
        d1.T,
        d2,
        d3,
        frame_grad.swapaxes(1, 2),
    )


def solution(mesh):
    placed = (
        P(("dp", "mp"), None, None),
        P(("dp", "mp"), None),
        P(),
        P(),
        P(),
        P("mp", None),
        P(),
        P(),
        P(),
        P("mp", "dp"),
        P("dp", None),
        P("dp", None),
    )
    return jax.shard_map(
        shards,
        mesh=mesh,
        in_specs=placed,
        out_specs=(
            P(("dp", "mp"), None, None),
            P(("dp", "mp"), None),
            P(("dp", "mp"), None),
            P(),
            P(),
            P(),
            P("mp", "dp"),
            P("dp", None),
            P("dp", None),
            P(("dp", "mp"), None, None),
        ),
        check_vma=False,
    )
```
